256 devices in a mesh: dp: 64 (over z, x, core), space: 2 (over y_hi), chan: 2 (over y_lo).
Axes of the slice: x: 4, y: 4 (y_hi: 2, y_lo: 2; y = y_hi * 2 + y_lo), z: 8, core: 2. Of those that a mesh axis runs over, the one named last changes fastest.
Arguments:
- images: bfloat16 [64, 32, 256, 512], P('dp', ('space', 'chan')), may hold values from -6 to 6
- reduce_weight: bfloat16 [512, 256], replicated, may hold values from -0.375 to 0.375
- spatial_weight: bfloat16 [3, 3, 256, 256], replicated, may hold values from -0.1875 to 0.1875
- expand_weight: bfloat16 [768, 1024], P(None, ('space', 'chan')), may hold values from -0.21875 to 0.21875
- cotangent: bfloat16 [64, 16, 128, 1024], P('dp', None, None, ('space', 'chan')), may hold values from -6 to 6
Outputs:
- output: bfloat16 [64, 16, 128, 1024], P('dp', None, None, ('space', 'chan'))
- input_grad: bfloat16 [64, 32, 256, 512], P('dp', ('space', 'chan'))
- reduce_grad: float32 [512, 256], replicated
- spatial_grad: float32 [3, 3, 256, 256], replicated
- expand_grad: float32 [768, 1024], P(None, ('space', 'chan'))
The draws below stay inside these ranges and needn't reach their ends.
All inputs are finite; a program needn't handle non-finite values.
Results may differ from the reference program's by a relative error of at most 0.0067.
Values may be sent and summed in bfloat16 or wider, within the bound.
A program may use at most 128 MiB of HBM per device.

```python
import math
import jax
import jax.numpy as jnp
from jax import lax

C_IN = 512
MID = 256
C_OUT = 1024
WIDTH = 256
SAMPLES = 64
ROWS = 32


def levels(key, shape, split, low, high):
    loudness = 1.0
    for position, blocks in split:
        steps = jax.random.uniform(jax.random.fold_in(jax.random.fold_in(key, 6), position), (blocks,), jnp.float32, low / len(split), high / len(split))
        loudness = loudness * jnp.repeat(jnp.exp(steps), shape[position] // blocks).reshape((-1,) + (1,) * (len(shape) - 1 - position))
    return loudness


def gaussian(own_key, shape, deviation, most, split=(), dtype=jnp.bfloat16):
    values = deviation * jax.random.normal(own_key, shape, jnp.float32)
    if split:
        values = values * levels(own_key, shape, split, -0.22, 0.18)
    return jnp.clip(values, -most, most).astype(dtype)


def setup_inputs(seed: int = 0) -> dict:
    keys = jax.random.split(jax.random.key(seed), 6)
    images = gaussian(keys[0], (SAMPLES, ROWS, WIDTH, C_IN), 1.0, 6.0, ((0, 64), (1, 4)))
    reduce_weight = gaussian(keys[1], (C_IN, MID), (C_IN // 2) ** -0.5, 0.375)
    spatial_weight = gaussian(keys[2], (3, 3, MID, MID), (9 * MID // 2) ** -0.5, 0.1875)
    expand_weight = gaussian(keys[3], (MID + C_IN, C_OUT), (MID + C_IN) ** -0.5, 0.21875, ((1, 4),))
    cotangent = gaussian(keys[4], (SAMPLES, ROWS // 2, WIDTH // 2, C_OUT), 1.0, 6.0, ((0, 64), (3, 4)))
    return {"images": images, "reduce_weight": reduce_weight, "spatial_weight": spatial_weight, "expand_weight": expand_weight, "cotangent": cotangent}


def silu_value(pre):
    return pre * jax.nn.sigmoid(pre)

def silu_slope(pre):
    sigma = jax.nn.sigmoid(pre)
    return sigma * (1.0 + pre * (1.0 - sigma))

def taps(padded, rows, cols):
    return [padded[row_off:row_off + rows:2, col_off:col_off + cols:2] for row_off in range(3) for col_off in range(3)]

def pad_axis(array, axis, before, after):
    widths = [(0, 0)] * array.ndim
    widths[axis] = (before, after)
    return jnp.pad(array, widths)

def weave_odd(even_part, odd_part, axis):
    odd_full = pad_axis(odd_part, axis, 0, 1)
    woven = jnp.stack([even_part, odd_full], axis=axis + 1)
    shape = list(even_part.shape)
    count = shape[axis]
    shape[axis] = 2 * count
    woven = woven.reshape(shape)
    return lax.slice_in_dim(woven, 0, 2 * count - 1, axis=axis)

def fold_taps(first, second, third, axis):
    even_part = pad_axis(first, axis, 0, 1) + pad_axis(third, axis, 1, 0)
    return weave_odd(even_part, second, axis)

def spread_back(grad_out, spatial_weight, rows, cols):
    columns_done = []
    for col_off in range(3):
        parts = [jnp.dot(grad_out, spatial_weight[row_off, col_off].T, preferred_element_type=jnp.float32) for row_off in range(3)]
        columns_done.append(fold_taps(parts[0], parts[1], parts[2], 0))
    return fold_taps(columns_done[0], columns_done[1], columns_done[2], 1)

def place_even(small):
    half_rows, half_cols, chans = small.shape
    empty = jnp.zeros_like(small)
    wide = jnp.stack([small, empty], axis=2).reshape(half_rows, 2 * half_cols, chans)
    return jnp.stack([wide, jnp.zeros_like(wide)], axis=1).reshape(2 * half_rows, 2 * half_cols, chans)

def sample_pass(image, cot_block, reduce_weight, spatial_weight, expand_weight):
    rows = image.shape[0]
    cols = image.shape[1]
    middle = reduce_weight.shape[1]
    reduce_pre = jnp.dot(image, reduce_weight, preferred_element_type=jnp.float32)
    reduced = silu_value(reduce_pre).astype(jnp.bfloat16)
    padded = jnp.pad(reduced, ((1, 0), (1, 0), (0, 0)))
    windows = taps(padded, rows, cols)
    spatial_pre = jnp.zeros((rows // 2, cols // 2, middle), jnp.float32)
    for tap_index in range(9):
        spatial_pre = spatial_pre + jnp.dot(windows[tap_index], spatial_weight[tap_index // 3, tap_index % 3], preferred_element_type=jnp.float32)
    spatial = silu_value(spatial_pre).astype(jnp.bfloat16)
    stacked = jnp.concatenate([spatial, image[::2, ::2]], axis=-1)
    expand_pre = jnp.dot(stacked, expand_weight, preferred_element_type=jnp.float32)
    output = silu_value(expand_pre).astype(jnp.bfloat16)
    grad_pre = (cot_block.astype(jnp.float32) * silu_slope(expand_pre)).astype(jnp.bfloat16)
    flat_in = stacked.reshape(-1, stacked.shape[-1])
    flat_grad = grad_pre.reshape(-1, grad_pre.shape[-1])
    expand_term = jnp.dot(flat_in.T, flat_grad, preferred_element_type=jnp.float32)
    stacked_grad = jnp.dot(grad_pre, expand_weight.T, preferred_element_type=jnp.float32)
    spatial_grad_pre = (stacked_grad[..., :middle] * silu_slope(spatial_pre)).astype(jnp.bfloat16)
    flat_spatial = spatial_grad_pre.reshape(-1, middle)
    spatial_term = jnp.stack([jnp.dot(window.reshape(-1, middle).T, flat_spatial, preferred_element_type=jnp.float32) for window in windows]).reshape(3, 3, middle, middle)
    canvas = spread_back(spatial_grad_pre, spatial_weight, rows, cols)
    reduce_grad_pre = (canvas[1:, 1:] * silu_slope(reduce_pre)).astype(jnp.bfloat16)
    reduce_term = jnp.dot(image.reshape(-1, image.shape[-1]).T, reduce_grad_pre.reshape(-1, middle), preferred_element_type=jnp.float32)
    input_full = jnp.dot(reduce_grad_pre, reduce_weight.T, preferred_element_type=jnp.float32)
    input_full = input_full + place_even(stacked_grad[..., middle:])
    return (output, input_full.astype(jnp.bfloat16), reduce_term, spatial_term, expand_term)

def reference(images, reduce_weight, spatial_weight, expand_weight, cotangent):

    def step_fn(carry, pair):
        image, cot_block = pair
        output, input_grad, reduce_term, spatial_term, expand_term = sample_pass(image, cot_block, reduce_weight, spatial_weight, expand_weight)
        carry = (carry[0] + reduce_term, carry[1] + spatial_term, carry[2] + expand_term)
        return (carry, (output, input_grad))
    start = (jnp.zeros((C_IN, MID), jnp.float32), jnp.zeros((3, 3, MID, MID), jnp.float32), jnp.zeros((MID + C_IN, C_OUT), jnp.float32))
    totals, results = lax.scan(step_fn, start, (images, cotangent))
    scale = 1.0 / math.sqrt(SAMPLES * (ROWS // 2) * (WIDTH // 2))
    return (results[0], results[1], totals[0] * scale, totals[1] * scale, totals[2] * scale)
```

```python
import functools
import math

import jax
import jax.numpy as jnp
from jax import lax
from jax.experimental import pallas as pl
from jax.experimental.pallas import tpu as pltpu
from jax.sharding import PartitionSpec as P

MESH = pl.DeviceIdType.MESH
F32 = jnp.float32
BF16 = jnp.bfloat16


def sigmoid(pre):
    return 1.0 / (1.0 + jnp.exp(-pre))


def slope_of(pre, sig):
    return sig * (1.0 + pre * (1.0 - sig))


def dot(left, right):
    return jnp.dot(left, right, preferred_element_type=F32)


def dot_tn(left, right):
    return lax.dot_general(left, right, (((0,), (0,)), ((), ())), preferred_element_type=F32)


def dot_nt(left, right):
    return lax.dot_general(left, right, (((1,), (1,)), ((), ())), preferred_element_type=F32)


def loop(low, high, step_fn):
    def step(index, carry):
        step_fn(index)
        return carry

    lax.fori_loop(low, high, step, 0)


def block_kernel(
    nx, nz, img, wr, ws, we, cot,
    out, igrad, rgrad, sgrad, egrad,
    wg, cotr, a_s, pre_s, rowbuf, spre_s, stk, obuf, stg, sgp, sgq, sbuf, rg_s, rgp_s, rterm, widebuf,
    e_send, e_rc, e_p, e_rp, e_z, e_rz, e_f, e_g, e_out,
    s_send, s_rc, s_p, s_rp, r_send, r_rc, r_p, r_rp, t_z, t_rz, t_f, t_g, t_out,
    y_send_sem, y_recv_sem, p_send_sem, p_recv_sem, z_send_sem, z_recv_sem, c_send_sem, c_recv_sem,
):
    rows, cols, chans = img.shape
    half_cols = cols // 2
    half_rows = rows // 2
    mid = wr.shape[1]
    stack_ch, filt = we.shape
    pix = half_rows * half_cols
    lanes = 128
    planes = nx * 4
    dp = lax.axis_index("dp")
    y = lax.axis_index("space") * 2 + lax.axis_index("chan")
    core = dp % 2
    x = (dp // 2) % nx
    z = dp // (2 * nx)
    plane = x * 4 + y
    scale = 1.0 / math.sqrt(lax.axis_size("dp") * cot.shape[0] * pix)

    def device(z_at, x_at, core_at, y_at):
        return ((z_at * nx + x_at) * 2 + core_at, y_at // 2, y_at % 2)

    def at_y(y_at):
        return device(z, x, core, y_at)

    def at_x(x_at):
        return device(z, x_at, core, y)

    def at_z(z_at):
        return device(z_at, x, core, y)

    def at_plane(place):
        return device(z, place // 4, core, place % 4)

    other_core = device(z, x, 1 - core, y)

    def remote(src, dst, send_sem, recv_sem, target):
        return pltpu.make_async_remote_copy(
            src_ref=src, dst_ref=dst, send_sem=send_sem, recv_sem=recv_sem, device_id=target, device_id_type=MESH
        )

    barrier = pltpu.get_barrier_semaphore()
    pl.semaphore_signal(barrier, inc=1, device_id=other_core, device_id_type=MESH)

    def greet_plane(k):
        pl.semaphore_signal(barrier, inc=1, device_id=at_plane((plane + k) % planes), device_id_type=MESH)

    def greet_z(k):
        pl.semaphore_signal(barrier, inc=1, device_id=at_z((z + k) % nz), device_id_type=MESH)

    loop(1, planes, greet_plane)
    loop(1, nz, greet_z)

    rowbuf[:, 0:8] = jnp.zeros((mid // lanes, 8, lanes), F32)

    def reduce_row(p):
        pre = dot(img[p], wr[...])
        pre_s[p] = pre
        reduced = pre * sigmoid(pre)
        a_par, a_idx = (p + 1) % 2, (p + 1) // 2
        for block in range(mid // lanes):
            rowbuf[block, 8 : 8 + cols] = reduced[:, block * lanes : (block + 1) * lanes]
            for part, start in enumerate((7, 8, 9)):
                lane = part * mid + block * lanes
                a_s[a_par, a_idx, :, lane : lane + lanes] = rowbuf[block, pl.ds(start, half_cols, stride=2), :].astype(BF16)

    reduce_row(rows - 1)
    pl.semaphore_wait(barrier, planes + nz - 1)

    halo_row = remote(
        a_s.at[0, half_rows], a_s.at[0, 0], y_send_sem.at[12], y_recv_sem.at[12], at_y((y + 1) % 4)
    )

    @pl.when(y < 3)
    def _():
        halo_row.start()

    part_rows = stack_ch // (2 * nx)
    part = pl.ds(pl.multiple_of((core * nx + x) * part_rows, part_rows), part_rows)
    half_part = pl.ds(pl.multiple_of(core * (stack_ch // 2), stack_ch // 2), stack_ch // 2)

    def weight_y(k):
        return remote(we.at[part], wg.at[k, part], y_send_sem.at[k], y_recv_sem.at[k], at_y((y + k) % 4))

    def weight_x(k):
        return remote(
            wg.at[1:4, part], wg.at[1:4, part], z_send_sem.at[3 * nz + k], z_recv_sem.at[3 * nz + k], at_x((x + k) % nx)
        )

    weight_core = remote(wg.at[1:4, half_part], wg.at[1:4, half_part], c_send_sem.at[0], c_recv_sem.at[0], other_core)

    def cot_y(k):
        return remote(
            cot.at[(y + k) % 4], cotr.at[k], y_send_sem.at[4 + k], y_recv_sem.at[4 + k], at_y((y + k) % 4)
        )

    loop(1, 4, lambda k: weight_y(k).start())
    loop(1, 4, lambda k: cot_y(k).start())

    wg[0] = we[...]
    cotr[0] = cot[y]
    loop(0, 2, reduce_row)
    loop(1, 4, lambda k: weight_y(k).wait_recv())
    loop(1, nx, lambda k: weight_x(k).start())
    loop(2, rows - 1, reduce_row)

    take = (
        lax.broadcasted_iota(jnp.int32, (half_cols, cols), 1)
        == 2 * lax.broadcasted_iota(jnp.int32, (half_cols, cols), 0)
    ).astype(F32).astype(BF16)

    def pick_even(i):
        stk[i, :, mid : mid + chans] = dot(take, img[2 * i]).astype(BF16)

    loop(0, half_rows, pick_even)

    @pl.when(y > 0)
    def _():
        halo_row.wait_recv()

    @pl.when(y == 0)
    def _():
        a_s[0, 0] = jnp.zeros_like(a_s[0, 0])

    def windows(r):
        return a_s[r % 2, r // 2 : r // 2 + half_rows].reshape(pix, 3 * mid)

    spre = dot(windows(0), ws[0])
    spre = spre + dot(windows(1), ws[1])
    spre = spre + dot(windows(2), ws[2])
    spre_s[...] = spre
    stk[:, :, 0:mid] = (spre * sigmoid(spre)).astype(BF16).reshape(half_rows, half_cols, mid)

    loop(1, nx, lambda k: weight_x(k).wait_recv())
    weight_core.start()
    weight_core.wait_recv()

    def out_y(k):
        return remote(
            obuf.at[k], out.at[y], y_send_sem.at[8 + k], y_recv_sem.at[8 + k], at_y((y + 4 - k) % 4)
        )

    e_rows = stack_ch // nx

    def expand_block(k):
        owner = (y + 4 - k) % 4
        stacked = stk[...].reshape(pix, stack_ch)
        pre = dot(stacked, wg[k])
        sig = sigmoid(pre)
        value = (pre * sig).astype(BF16)

        @pl.when(k == 0)
        def _():
            out[y] = value

        @pl.when(k > 0)
        def _():
            obuf[k] = value
            out_y(k).start()
            cot_y(k).wait_recv()

        grad = (cotr[k].astype(F32) * slope_of(pre, sig)).astype(BF16)
        term = dot_tn(stacked, grad).astype(BF16)
        for h in range(2):
            for x_at in range(nx):
                e_send[h, x_at * 4 + owner] = term[x_at * e_rows : (x_at + 1) * e_rows, h * lanes : (h + 1) * lanes]
        back = dot_nt(grad, wg[k])

        @pl.when(k == 0)
        def _():
            stg[...] = back

        @pl.when(k > 0)
        def _():
            stg[...] += back

    loop(0, 4, expand_block)

    def core_sum(send, got, k):
        return remote(send.at[1 - core], got, c_send_sem.at[k], c_recv_sem.at[k], other_core)

    def plane_sum(summed, got, group, k):
        slot = group * planes + k
        place = (plane + k) % planes
        return remote(
            summed.at[place], got.at[k], p_send_sem.at[slot], p_recv_sem.at[slot], at_plane(place)
        )

    def add_core(send, got, summed):
        def one(q):
            summed[q] = (send[core, q].astype(F32) + got[q].astype(F32)).astype(BF16)

        loop(0, planes, one)

    def plane_total(summed, got, group):
        def one(k, total):
            plane_sum(summed, got, group, k).wait_recv()
            return total + got[k].astype(F32)

        return lax.fori_loop(1, planes, one, summed[plane].astype(F32))

    e_core = core_sum(e_send, e_rc, 1)
    e_core.start()

    spre = spre_s[...]
    sig = sigmoid(spre)
    sgrad_pre = stg[:, 0:mid] * slope_of(spre, sig)
    sgp[0:half_rows] = sgrad_pre.astype(BF16).reshape(half_rows, half_cols, mid)
    halo_grad = remote(sgp.at[0], sgp.at[half_rows], y_send_sem.at[13], y_recv_sem.at[13], at_y((y + 3) % 4))

    @pl.when(y > 0)
    def _():
        halo_grad.start()

    s_rows = mid * 3 // planes
    flat = sgp[0:half_rows].reshape(pix, mid)
    for r in range(3):
        term = dot_tn(windows(r), flat).astype(BF16)
        for h in range(2):
            for q in range(planes):
                s_send[h, q, r * s_rows : (r + 1) * s_rows] = term[
                    q * s_rows : (q + 1) * s_rows, h * lanes : (h + 1) * lanes
                ]
    s_core = core_sum(s_send, s_rc, 2)
    s_core.start()
    e_core.wait_recv()
    add_core(e_send, e_rc, e_p)
    loop(1, planes, lambda k: plane_sum(e_p, e_rp, 0, k).start())

    @pl.when(y < 3)
    def _():
        halo_grad.wait_recv()

    @pl.when(y == 3)
    def _():
        sgp[half_rows] = jnp.zeros_like(sgp[half_rows])

    sbuf[half_cols : half_cols + 8] = jnp.zeros((8, mid), F32)

    def shift_row(i):
        sbuf[0:half_cols] = sgp[i].astype(F32)
        sgq[i] = sbuf[1 : 1 + half_cols].astype(BF16)

    loop(0, half_rows + 1, shift_row)
    here = sgp[0:half_rows].reshape(pix, mid)
    here_next = sgq[0:half_rows].reshape(pix, mid)

    def weave(row_par, col_par, value):
        value = value.reshape(half_rows, half_cols, mid)
        for i in range(half_rows):
            for block in range(mid // lanes):
                rg_s[2 * i + row_par, block, pl.ds(col_par, half_cols, stride=2), :] = value[
                    i, :, block * lanes : (block + 1) * lanes
                ]

    def tap(r, c):
        return ws[r, c * mid : (c + 1) * mid, :]

    weave(0, 0, dot_nt(here, tap(1, 1)))
    weave(0, 1, dot_nt(here, tap(1, 2)) + dot_nt(here_next, tap(1, 0)))
    below = sgp[1 : half_rows + 1].reshape(pix, mid)
    below_next = sgq[1 : half_rows + 1].reshape(pix, mid)
    weave(1, 0, dot_nt(here, tap(2, 1)) + dot_nt(below, tap(0, 1)))
    weave(
        1, 1,
        dot_nt(here, tap(2, 2)) + dot_nt(here_next, tap(2, 0)) + dot_nt(below, tap(0, 2)) + dot_nt(below_next, tap(0, 0)),
    )
    s_core.wait_recv()
    add_core(s_send, s_rc, s_p)
    loop(1, planes, lambda k: plane_sum(s_p, s_rp, 1, k).start())

    rterm[...] = jnp.zeros_like(rterm)

    def reduce_back(p):
        pre = pre_s[p]
        canvas = jnp.concatenate([rg_s[p, block] for block in range(mid // lanes)], axis=1)
        grad = (canvas * slope_of(pre, sigmoid(pre))).astype(BF16)
        rgp_s[p] = grad
        rterm[...] += dot_tn(img[p], grad)

    loop(0, rows, reduce_back)
    r_rows = chans // planes
    for h in range(2):
        for q in range(planes):
            r_send[h, q] = rterm[q * r_rows : (q + 1) * r_rows, h * lanes : (h + 1) * lanes].astype(BF16)
    r_core = core_sum(r_send, r_rc, 3)
    r_core.start()

    e_z[...] = plane_total(e_p, e_rp, 0).reshape(e_z.shape)

    def z_sum(src, dst, group, k):
        slot = group * nz + k
        return remote(
            src.at[(z + k) % nz], dst.at[k], z_send_sem.at[slot], z_recv_sem.at[slot], at_z((z + k) % nz)
        )

    def z_spread(src, dst, group, k):
        slot = group * nz + k
        return remote(src, dst.at[z], z_send_sem.at[slot], z_recv_sem.at[slot], at_z((z + k) % nz))

    def z_total(src, dst, group):
        def one(k, total):
            z_sum(src, dst, group, k).wait_recv()
            return total + dst[k]

        return lax.fori_loop(1, nz, one, src[z])

    loop(1, nz, lambda k: z_sum(e_z, e_rz, 0, k).start())

    r_core.wait_recv()
    add_core(r_send, r_rc, r_p)
    loop(1, planes, lambda k: plane_sum(r_p, r_rp, 2, k).start())

    e_f[...] = z_total(e_z, e_rz, 0)
    loop(1, nz, lambda k: z_spread(e_f, e_g, 1, k).start())

    def input_row(p):
        wide = dot_nt(rgp_s[p], wr[...])

        @pl.when(p % 2 == 1)
        def _():
            igrad[p] = wide.astype(BF16)

        @pl.when(p % 2 == 0)
        def _():
            first = pl.ds(pl.multiple_of((p // 2) * half_cols, half_cols), half_cols)
            for block in range(chans // lanes):
                lane = slice(block * lanes, (block + 1) * lanes)
                widebuf[block] = wide[:, lane]
                widebuf[block, pl.ds(0, half_cols, stride=2), :] = (
                    widebuf[block, pl.ds(0, half_cols, stride=2), :]
                    + stg[first, mid + block * lanes : mid + (block + 1) * lanes]
                )
                igrad[p, :, lane] = widebuf[block].astype(BF16)

    loop(0, rows, input_row)

    st_rows, rt_rows, t_rows = 3 * s_rows, r_rows, t_z.shape[0] * t_z.shape[1]
    total = [plane_total(s_p, s_rp, 1), plane_total(r_p, r_rp, 2)]
    if t_rows > st_rows + rt_rows:
        total.append(jnp.zeros((t_rows - st_rows - rt_rows, lanes), F32))
    t_z[...] = jnp.concatenate(total, axis=0).reshape(t_z.shape)
    loop(1, nz, lambda k: z_sum(t_z, t_rz, 2, k).start())

    loop(1, nz, lambda k: z_spread(e_f, e_g, 1, k).wait_recv())
    e_g[z] = e_f[...]
    e_out[core, x] = e_g[...].reshape(e_rows, lanes).astype(BF16)

    def e_x(k):
        return remote(
            e_out.at[core, x], e_out.at[core, x], p_send_sem.at[3 * planes + k], p_recv_sem.at[3 * planes + k], at_x((x + k) % nx)
        )

    loop(1, nx, lambda k: e_x(k).start())

    t_f[...] = z_total(t_z, t_rz, 2)
    loop(1, nz, lambda k: z_spread(t_f, t_g, 4, k).start())
    loop(1, nx, lambda k: e_x(k).wait_recv())
    e_cross = remote(e_out.at[core], e_out.at[core], c_send_sem.at[4], c_recv_sem.at[4], other_core)
    loop(1, nx, lambda k: e_x(k).wait_send())
    e_cross.start()

    loop(1, nz, lambda k: z_spread(t_f, t_g, 4, k).wait_recv())
    t_g[z] = t_f[...]
    t_out[core, plane] = t_g[...].reshape(t_rows, lanes).astype(BF16)

    def t_spread(k):
        slot = 4 * planes + k
        return remote(
            t_out.at[core, plane], t_out.at[core, plane], p_send_sem.at[slot], p_recv_sem.at[slot], at_plane((plane + k) % planes)
        )

    def t_cross(k):
        place = (plane + planes - k) % planes
        return remote(
            t_out.at[core, place], t_out.at[core, place], c_send_sem.at[5 + k], c_recv_sem.at[5 + k], other_core
        )

    loop(1, planes, lambda k: t_spread(k).start())
    t_cross(0).start()

    def pass_on(k):
        t_spread(k).wait_recv()
        t_cross(k).start()

    loop(1, planes, pass_on)
    e_cross.wait_recv()
    for h in range(2):
        for x_at in range(nx):
            egrad[x_at * e_rows : (x_at + 1) * e_rows, h * lanes : (h + 1) * lanes] = e_out[h, x_at].astype(F32) * scale
    loop(0, planes, lambda k: t_cross(k).wait_recv())
    for h in range(2):
        lane = slice(h * lanes, (h + 1) * lanes)
        for q in range(planes):
            for r in range(3):
                sgrad[r, q * s_rows : (q + 1) * s_rows, lane] = t_out[h, q, r * s_rows : (r + 1) * s_rows].astype(F32) * scale
            rgrad[q * r_rows : (q + 1) * r_rows, lane] = t_out[h, q, st_rows : st_rows + r_rows].astype(F32) * scale

    @pl.when(y < 3)
    def _():
        halo_row.wait_send()

    @pl.when(y > 0)
    def _():
        halo_grad.wait_send()

    def finish_y(k):
        weight_y(k).wait_send()
        cot_y(k).wait_send()
        out_y(k).wait()

    loop(1, 4, finish_y)
    loop(1, nx, lambda k: weight_x(k).wait_send())
    for copy in (weight_core, e_core, s_core, r_core, e_cross):
        copy.wait_send()

    def finish_plane(k):
        plane_sum(e_p, e_rp, 0, k).wait_send()
        plane_sum(s_p, s_rp, 1, k).wait_send()
        plane_sum(r_p, r_rp, 2, k).wait_send()
        t_spread(k).wait_send()

    loop(1, planes, finish_plane)

    def finish_z(k):
        z_sum(e_z, e_rz, 0, k).wait_send()
        z_spread(e_f, e_g, 1, k).wait_send()
        z_sum(t_z, t_rz, 2, k).wait_send()
        z_spread(t_f, t_g, 4, k).wait_send()

    loop(1, nz, finish_z)
    loop(0, planes, lambda k: t_cross(k).wait_send())


def body(nx, nz, images, reduce_weight, spatial_weight, expand_weight, cotangent):
    image = images[0]
    rows, cols, chans = image.shape
    mid = reduce_weight.shape[1]
    stack_ch, filt = expand_weight.shape
    half_rows, half_cols = rows // 2, cols // 2
    pix = half_rows * half_cols
    planes = nx * 4
    lanes = 128
    e_rows = stack_ch // nx
    s_rows = 9 * mid // planes
    r_rows = chans // planes
    t_rows = -(-(s_rows + r_rows) // (8 * nz)) * 8 * nz
    cot_blocks = cotangent[0].reshape(4, pix, filt)
    weights = spatial_weight.reshape(3, 3 * mid, mid)
    vmem = pl.BlockSpec(memory_space=pltpu.VMEM)
    V = pltpu.VMEM
    D = pltpu.SemaphoreType.DMA
    scratch = [
        V((4, stack_ch, filt), BF16),
        V((4, pix, filt), BF16),
        V((2, half_rows + 1, half_cols, 3 * mid), BF16),
        V((rows, cols, mid), F32),
        V((mid // lanes, cols + 16, lanes), F32),
        V((pix, mid), F32),
        V((half_rows, half_cols, stack_ch), BF16),
        V((4, pix, filt), BF16),
        V((pix, stack_ch), F32),
        V((half_rows + 1, half_cols, mid), BF16),
        V((half_rows + 1, half_cols, mid), BF16),
        V((half_cols + 8, mid), F32),
        V((rows, mid // lanes, cols, lanes), F32),
        V((rows, cols, mid), BF16),
        V((chans, mid), F32),
        V((chans // lanes, cols, lanes), F32),
        V((2, planes, e_rows, lanes), BF16),
        V((planes, e_rows, lanes), BF16),
        V((planes, e_rows, lanes), BF16),
        V((planes, e_rows, lanes), BF16),
        V((nz, e_rows // nz, lanes), F32),
        V((nz, e_rows // nz, lanes), F32),
        V((e_rows // nz, lanes), F32),
        V((nz, e_rows // nz, lanes), F32),
        V((2, nx, e_rows, lanes), BF16),
        V((2, planes, s_rows, lanes), BF16),
        V((planes, s_rows, lanes), BF16),
        V((planes, s_rows, lanes), BF16),
        V((planes, s_rows, lanes), BF16),
        V((2, planes, r_rows, lanes), BF16),
        V((planes, r_rows, lanes), BF16),
        V((planes, r_rows, lanes), BF16),
        V((planes, r_rows, lanes), BF16),
        V((nz, t_rows // nz, lanes), F32),
        V((nz, t_rows // nz, lanes), F32),
        V((t_rows // nz, lanes), F32),
        V((nz, t_rows // nz, lanes), F32),
        V((2, planes, t_rows, lanes), BF16),
        D((14,)),
        D((14,)),
        D((5 * planes,)),
        D((5 * planes,)),
        D((5 * nz,)),
        D((5 * nz,)),
        D((5 + planes,)),
        D((5 + planes,)),
    ]
    output, input_grad, reduce_grad, spatial_grad, expand_grad = pl.pallas_call(
        functools.partial(block_kernel, nx, nz),
        out_shape=(
            jax.ShapeDtypeStruct((4, pix, filt), BF16),
            jax.ShapeDtypeStruct(image.shape, BF16),
            jax.ShapeDtypeStruct((chans, mid), F32),
            jax.ShapeDtypeStruct((3, 3 * mid, mid), F32),
            jax.ShapeDtypeStruct((stack_ch, filt), F32),
        ),
        in_specs=[vmem] * 5,
        out_specs=[vmem] * 5,
        scratch_shapes=scratch,
        compiler_params=pltpu.CompilerParams(
            collective_id=0, has_side_effects=True, vmem_limit_bytes=56 * 1024 * 1024
        ),
    )(image, reduce_weight, weights, expand_weight, cot_blocks)
    return (
        output.reshape((1, 4 * half_rows, half_cols, filt)),
        input_grad[None],
        reduce_grad,
        spatial_grad.reshape(3, 3, mid, mid),
        expand_grad,
    )


def solution(mesh):
    nx = 4 if mesh.shape["dp"] >= 32 else 2
    nz = mesh.shape["dp"] // (2 * nx)
    return jax.shard_map(
        functools.partial(body, nx, nz),
        mesh=mesh,
        in_specs=(
            P("dp", ("space", "chan"), None, None),
            P(),
            P(),
            P(None, ("space", "chan")),
            P("dp", None, None, ("space", "chan")),
        ),
        out_specs=(
            P("dp", None, None, ("space", "chan")),
            P("dp", ("space", "chan"), None, None),
            P(),
            P(),
            P(None, ("space", "chan")),
        ),
        check_vma=False,
    )
```

```python
import functools
import math

import jax
import jax.numpy as jnp
from jax import lax
from jax.experimental import pallas as pl
from jax.experimental.pallas import tpu as pltpu
from jax.sharding import PartitionSpec as P

MESH = pl.DeviceIdType.MESH
F32 = jnp.float32
BF16 = jnp.bfloat16


def sigmoid(pre):
    return 1.0 / (1.0 + jnp.exp(-pre))


def slope_of(pre, sig):
    return sig * (1.0 + pre * (1.0 - sig))


def dot(left, right):
    return jnp.dot(left, right, preferred_element_type=F32)


def dot_tn(left, right):
    return lax.dot_general(left, right, (((0,), (0,)), ((), ())), preferred_element_type=F32)


def dot_nt(left, right):
    return lax.dot_general(left, right, (((1,), (1,)), ((), ())), preferred_element_type=F32)


def loop(low, high, step_fn):
    def step(index, carry):
        step_fn(index)
        return carry

    lax.fori_loop(low, high, step, 0)


def block_kernel(
    nx, nz, img_hbm, wr_hbm, ws_hbm, we, cot,
    out, igrad, rgrad, sgrad, egrad,
    img, wr, ws, slp, wg, cotr, a_s, pre_s, rowbuf, spre_s, stk, obuf, stg, sgp, sgq, sbuf, rg_s, rgp_s, rterm, widebuf,
    e_send, e_rc, e_p, e_rp, e_z, e_rz, e_f, e_g, e_out,
    s_send, s_rc, s_p, s_rp, r_send, r_rc, r_p, r_rp, t_z, t_rz, t_f, t_g, t_out,
    y_send_sem, y_recv_sem, p_send_sem, p_recv_sem, z_send_sem, z_recv_sem, c_send_sem, c_recv_sem, w_send_sem, w_recv_sem, load_sem,
):
    rows, cols, chans = img.shape
    half_cols = cols // 2
    half_rows = rows // 2
    mid = wr.shape[1]
    stack_ch, filt = we.shape
    pix = half_rows * half_cols
    lanes = 128
    planes = nx * 4
    dp = lax.axis_index("dp")
    y = lax.axis_index("space") * 2 + lax.axis_index("chan")
    core = dp % 2
    x = (dp // 2) % nx
    z = dp // (2 * nx)
    plane = x * 4 + y
    scale = 1.0 / math.sqrt(lax.axis_size("dp") * cot.shape[0] * pix)

    def device(z_at, x_at, core_at, y_at):
        return ((z_at * nx + x_at) * 2 + core_at, y_at // 2, y_at % 2)

    def at_y(y_at):
        return device(z, x, core, y_at)

    def at_x(x_at):
        return device(z, x_at, core, y)

    def at_z(z_at):
        return device(z_at, x, core, y)

    def at_plane(place):
        return device(z, place // 4, core, place % 4)

    other_core = device(z, x, 1 - core, y)

    def remote(src, dst, send_sem, recv_sem, target):
        return pltpu.make_async_remote_copy(
            src_ref=src, dst_ref=dst, send_sem=send_sem, recv_sem=recv_sem, device_id=target, device_id_type=MESH
        )

    barrier = pltpu.get_barrier_semaphore()
    pl.semaphore_signal(barrier, inc=1, device_id=other_core, device_id_type=MESH)

    def greet_plane(k):
        pl.semaphore_signal(barrier, inc=1, device_id=at_plane((plane + k) % planes), device_id_type=MESH)

    def greet_z(k):
        pl.semaphore_signal(barrier, inc=1, device_id=at_z((z + k) % nz), device_id_type=MESH)

    loop(1, planes, greet_plane)
    loop(1, nz, greet_z)

    load_wr = pltpu.make_async_copy(wr_hbm, wr, load_sem.at[rows])
    load_ws = pltpu.make_async_copy(ws_hbm, ws, load_sem.at[rows + 1])
    load_we = pltpu.make_async_copy(we, wg.at[0], load_sem.at[rows + 2])
    load_cot = pltpu.make_async_copy(cot.at[y], cotr.at[0], load_sem.at[rows + 3])

    def load_row(p):
        return pltpu.make_async_copy(img_hbm.at[p], img.at[p], load_sem.at[p])

    load_wr.start()
    loop(0, rows, lambda p: load_row(p).start())
    load_ws.start()
    load_we.start()
    load_cot.start()

    rowbuf[:, 0:8] = jnp.zeros((mid // lanes, 8, lanes), F32)

    def reduce_row(p):
        load_row(p).wait()
        pre = dot(img[p], wr[...])
        pre_s[p] = pre
        reduced = pre * sigmoid(pre)
        a_par, a_idx = (p + 1) % 2, (p + 1) // 2
        for block in range(mid // lanes):
            rowbuf[block, 8 : 8 + cols] = reduced[:, block * lanes : (block + 1) * lanes]
            for part, start in enumerate((7, 8, 9)):
                lane = part * mid + block * lanes
                a_s[a_par, a_idx, :, lane : lane + lanes] = rowbuf[block, pl.ds(start, half_cols, stride=2), :].astype(BF16)

    load_wr.wait()
    loop(0, rows, reduce_row)
    pl.semaphore_wait(barrier, planes + nz - 1)

    part_rows = stack_ch // (2 * nx)
    part = pl.ds(pl.multiple_of((core * nx + x) * part_rows, part_rows), part_rows)
    half_part = pl.ds(pl.multiple_of(core * (stack_ch // 2), stack_ch // 2), stack_ch // 2)

    def weight_y(k):
        return remote(we.at[part], wg.at[k, part], y_send_sem.at[k], y_recv_sem.at[k], at_y((y + k) % 4))

    def weight_x(k, j):
        slot = k * nx + j
        return remote(wg.at[k, part], wg.at[k, part], w_send_sem.at[slot], w_recv_sem.at[slot], at_x((x + j) % nx))

    def weight_core(k):
        return remote(wg.at[k, half_part], wg.at[k, half_part], c_send_sem.at[k], c_recv_sem.at[k], other_core)

    def cot_y(k):
        return remote(
            cot.at[(y + k) % 4], cotr.at[k], y_send_sem.at[4 + k], y_recv_sem.at[4 + k], at_y((y + k) % 4)
        )

    def halo_part(index):
        return a_s.at[0, index, :, mid : 3 * mid]

    halo_row = remote(
        halo_part(half_rows), halo_part(0), y_send_sem.at[12], y_recv_sem.at[12], at_y((y + 1) % 4)
    )
    for k in (1, 3, 2):
        weight_y(k).start()

    @pl.when(y < 3)
    def _():
        halo_row.start()

    for k in (1, 3, 2):
        cot_y(k).start()

    take = (
        lax.broadcasted_iota(jnp.int32, (half_cols, cols), 1)
        == 2 * lax.broadcasted_iota(jnp.int32, (half_cols, cols), 0)
    ).astype(F32).astype(BF16)

    def pick_even(i):
        stk[i, :, mid : mid + chans] = dot(take, img[2 * i]).astype(BF16)

    loop(0, half_rows, pick_even)

    def windows(r):
        return a_s[r % 2, r // 2 : r // 2 + half_rows].reshape(pix, 3 * mid)

    load_ws.wait()
    spre_s[...] = dot(windows(1), ws[1]) + dot(windows(2), ws[2])
    for k in (1, 3, 2):
        weight_y(k).wait_recv()
        loop(1, nx, lambda j: weight_x(k, j).start())

    @pl.when(y > 0)
    def _():
        halo_row.wait_recv()
        sbuf[0:8] = jnp.zeros((8, mid), F32)
        sbuf[8 : 8 + half_cols] = a_s[0, 0, :, 2 * mid : 3 * mid].astype(F32)
        a_s[0, 0, :, 0:mid] = sbuf[7 : 7 + half_cols].astype(BF16)

    @pl.when(y == 0)
    def _():
        a_s[0, 0] = jnp.zeros_like(a_s[0, 0])

    spre = spre_s[...] + dot(windows(0), ws[0])
    spre_s[...] = spre
    stk[:, :, 0:mid] = (spre * sigmoid(spre)).astype(BF16).reshape(half_rows, half_cols, mid)

    def out_y(k):
        return remote(
            obuf.at[k], out.at[y], y_send_sem.at[8 + k], y_recv_sem.at[8 + k], at_y((y + 4 - k) % 4)
        )

    def expand_block(k):
        pre = dot(stk[...].reshape(pix, stack_ch), wg[k])
        sig = sigmoid(pre)
        value = (pre * sig).astype(BF16)
        slp[k] = slope_of(pre, sig)
        if k == 0:
            out[y] = value
        else:
            obuf[k] = value

    def weight_relay(k):
        loop(1, nx, lambda j: weight_x(k, j).wait_recv())
        weight_core(k).start()

    e_rows = stack_ch // nz

    def expand_back(k):
        owner = (y + 4 - k) % 4
        grad = (cotr[k].astype(F32) * slp[k]).astype(BF16)
        term = dot_tn(stk[...].reshape(pix, stack_ch), grad).astype(BF16)
        for h in range(2):
            for z_at in range(nz):
                e_send[h, z_at, owner] = term[z_at * e_rows : (z_at + 1) * e_rows, h * lanes : (h + 1) * lanes]
        back = dot_nt(grad, wg[k])
        if k == 0:
            stg[...] = back
        else:
            stg[...] += back

    load_we.wait()
    load_cot.wait()
    expand_block(0)
    weight_relay(1)
    expand_back(0)
    weight_relay(3)
    weight_core(1).wait_recv()
    expand_block(1)
    weight_relay(2)
    weight_core(3).wait_recv()
    expand_block(3)
    cot_y(1).wait_recv()
    expand_back(1)
    weight_core(2).wait_recv()
    expand_block(2)
    cot_y(3).wait_recv()
    expand_back(3)
    cot_y(2).wait_recv()
    out_y(1).start()
    out_y(3).start()
    expand_back(2)

    def core_sum(send, got, k):
        return remote(send.at[1 - core], got, c_send_sem.at[k], c_recv_sem.at[k], other_core)

    def plane_sum(summed, got, group, k):
        slot = group * planes + k
        place = (plane + k) % planes
        return remote(
            summed.at[place], got.at[k], p_send_sem.at[slot], p_recv_sem.at[slot], at_plane(place)
        )

    def add_core(send, got, summed):
        def one(q):
            summed[q] = (send[core, q].astype(F32) + got[q].astype(F32)).astype(BF16)

        loop(0, summed.shape[0], one)

    def plane_total(summed, got, group):
        def one(k, total):
            plane_sum(summed, got, group, k).wait_recv()
            return total + got[k].astype(F32)

        return lax.fori_loop(1, planes, one, summed[plane].astype(F32))

    def z_sum(src, dst, group, k):
        slot = group * nz + k
        return remote(
            src.at[(z + k) % nz], dst.at[k], z_send_sem.at[slot], z_recv_sem.at[slot], at_z((z + k) % nz)
        )

    def z_spread(src, dst, group, k):
        slot = group * nz + k
        return remote(src, dst.at[z], z_send_sem.at[slot], z_recv_sem.at[slot], at_z((z + k) % nz))

    def z_total(src, dst, group):
        def one(k, total):
            z_sum(src, dst, group, k).wait_recv()
            return total + dst[k].astype(F32)

        return lax.fori_loop(1, nz, one, src[z].astype(F32))

    e_core = core_sum(e_send, e_rc, 4)
    e_core.start()

    spre = spre_s[...]
    sig = sigmoid(spre)
    sgrad_pre = stg[:, 0:mid] * slope_of(spre, sig)
    sgp[0:half_rows] = sgrad_pre.astype(BF16).reshape(half_rows, half_cols, mid)
    halo_grad = remote(sgp.at[0], sgp.at[half_rows], y_send_sem.at[13], y_recv_sem.at[13], at_y((y + 3) % 4))

    @pl.when(y > 0)
    def _():
        halo_grad.start()

    s_rows = mid * 3 // planes
    flat = sgp[0:half_rows].reshape(pix, mid)
    for r in range(3):
        term = dot_tn(windows(r), flat).astype(BF16)
        for h in range(2):
            for q in range(planes):
                s_send[h, q, r * s_rows : (r + 1) * s_rows] = term[
                    q * s_rows : (q + 1) * s_rows, h * lanes : (h + 1) * lanes
                ]
    s_core = core_sum(s_send, s_rc, 5)
    s_core.start()
    e_core.wait_recv()
    add_core(e_send, e_rc, e_p)
    loop(1, nz, lambda k: z_sum(e_p, e_rp, 0, k).start())
    s_core.wait_recv()
    add_core(s_send, s_rc, s_p)
    loop(1, planes, lambda k: plane_sum(s_p, s_rp, 1, k).start())

    @pl.when(y < 3)
    def _():
        halo_grad.wait_recv()

    @pl.when(y == 3)
    def _():
        sgp[half_rows] = jnp.zeros_like(sgp[half_rows])

    sbuf[half_cols : half_cols + 8] = jnp.zeros((8, mid), F32)

    def shift_row(i):
        sbuf[0:half_cols] = sgp[i].astype(F32)
        sgq[i] = sbuf[1 : 1 + half_cols].astype(BF16)

    loop(0, half_rows + 1, shift_row)
    here = sgp[0:half_rows].reshape(pix, mid)
    here_next = sgq[0:half_rows].reshape(pix, mid)

    def weave(row_par, col_par, value):
        value = value.reshape(half_rows, half_cols, mid)
        for i in range(half_rows):
            for block in range(mid // lanes):
                rg_s[2 * i + row_par, block, pl.ds(col_par, half_cols, stride=2), :] = value[
                    i, :, block * lanes : (block + 1) * lanes
                ]

    def tap(r, c):
        return ws[r, c * mid : (c + 1) * mid, :]

    weave(0, 0, dot_nt(here, tap(1, 1)))
    weave(0, 1, dot_nt(here, tap(1, 2)) + dot_nt(here_next, tap(1, 0)))
    below = sgp[1 : half_rows + 1].reshape(pix, mid)
    below_next = sgq[1 : half_rows + 1].reshape(pix, mid)
    weave(1, 0, dot_nt(here, tap(2, 1)) + dot_nt(below, tap(0, 1)))
    weave(
        1, 1,
        dot_nt(here, tap(2, 2)) + dot_nt(here_next, tap(2, 0)) + dot_nt(below, tap(0, 2)) + dot_nt(below_next, tap(0, 0)),
    )
    rterm[...] = jnp.zeros_like(rterm)

    def reduce_back(p):
        pre = pre_s[p]
        canvas = jnp.concatenate([rg_s[p, block] for block in range(mid // lanes)], axis=1)
        grad = (canvas * slope_of(pre, sigmoid(pre))).astype(BF16)
        rgp_s[p] = grad
        rterm[...] += dot_tn(img[p], grad)

    loop(0, rows, reduce_back)
    r_rows = chans // planes
    for h in range(2):
        for q in range(planes):
            r_send[h, q] = rterm[q * r_rows : (q + 1) * r_rows, h * lanes : (h + 1) * lanes].astype(BF16)
    r_core = core_sum(r_send, r_rc, 6)
    r_core.start()

    out_y(2).start()
    r_core.wait_recv()
    add_core(r_send, r_rc, r_p)
    loop(1, planes, lambda k: plane_sum(r_p, r_rp, 2, k).start())

    def input_row(p):
        wide = dot_nt(rgp_s[p], wr[...])

        @pl.when(p % 2 == 1)
        def _():
            igrad[p] = wide.astype(BF16)

        @pl.when(p % 2 == 0)
        def _():
            first = pl.ds(pl.multiple_of((p // 2) * half_cols, half_cols), half_cols)
            for block in range(chans // lanes):
                lane = slice(block * lanes, (block + 1) * lanes)
                widebuf[block] = wide[:, lane]
                widebuf[block, pl.ds(0, half_cols, stride=2), :] = (
                    widebuf[block, pl.ds(0, half_cols, stride=2), :]
                    + stg[first, mid + block * lanes : mid + (block + 1) * lanes]
                )
                igrad[p, :, lane] = widebuf[block].astype(BF16)

    loop(0, rows, input_row)

    st_rows, rt_rows, t_rows = 3 * s_rows, r_rows, t_z.shape[0] * t_z.shape[1]
    total = [plane_total(s_p, s_rp, 1), plane_total(r_p, r_rp, 2)]
    if t_rows > st_rows + rt_rows:
        total.append(jnp.zeros((t_rows - st_rows - rt_rows, lanes), F32))
    t_z[...] = jnp.concatenate(total, axis=0).reshape(t_z.shape)
    loop(1, nz, lambda k: z_sum(t_z, t_rz, 2, k).start())

    e_z[...] = z_total(e_p, e_rp, 0).reshape(e_z.shape)

    def e_plane(k):
        place = (plane + k) % planes
        return remote(
            e_z.at[place % 4, place // 4], e_rz.at[k], p_send_sem.at[k], p_recv_sem.at[k], at_plane(place)
        )

    loop(1, planes, lambda k: e_plane(k).start())

    t_f[...] = z_total(t_z, t_rz, 2)
    loop(1, nz, lambda k: z_spread(t_f, t_g, 4, k).start())

    def e_total(k, total):
        e_plane(k).wait_recv()
        return total + e_rz[k]

    e_f[...] = lax.fori_loop(1, planes, e_total, e_z[y, x])

    def e_x(k):
        return remote(
            e_f, e_g.at[x], p_send_sem.at[3 * planes + k], p_recv_sem.at[3 * planes + k], at_x((x + k) % nx)
        )

    loop(1, nx, lambda k: e_x(k).start())

    loop(1, nz, lambda k: z_spread(t_f, t_g, 4, k).wait_recv())
    t_g[z] = t_f[...]
    t_out[core, plane] = t_g[...].reshape(t_rows, lanes).astype(BF16)

    def t_spread(k):
        slot = 4 * planes + k
        return remote(
            t_out.at[core, plane], t_out.at[core, plane], p_send_sem.at[slot], p_recv_sem.at[slot], at_plane((plane + k) % planes)
        )

    def t_cross(k):
        place = (plane + planes - k) % planes
        return remote(
            t_out.at[core, place], t_out.at[core, place], c_send_sem.at[8 + k], c_recv_sem.at[8 + k], other_core
        )

    loop(1, planes, lambda k: t_spread(k).start())
    t_cross(0).start()

    loop(1, nx, lambda k: e_x(k).wait_recv())
    e_g[x] = e_f[...]
    e_out[core, z] = e_g[...].reshape(e_rows, lanes).astype(BF16)

    def e_back(k):
        slot = nz + k
        return remote(
            e_out.at[core, z], e_out.at[core, z], z_send_sem.at[slot], z_recv_sem.at[slot], at_z((z + k) % nz)
        )

    loop(1, nz, lambda k: e_back(k).start())

    def pass_on(k):
        t_spread(k).wait_recv()
        t_cross(k).start()

    loop(1, planes, pass_on)
    loop(1, nz, lambda k: e_back(k).wait())
    e_cross = remote(e_out.at[core], e_out.at[core], c_send_sem.at[7], c_recv_sem.at[7], other_core)
    e_cross.start()

    def finish_place(h, q):
        lane = slice(h * lanes, (h + 1) * lanes)
        for r in range(3):
            rows_at = pl.ds(pl.multiple_of(q * s_rows, s_rows), s_rows)
            sgrad[r, rows_at, lane] = t_out[h, q, r * s_rows : (r + 1) * s_rows].astype(F32) * scale
        rows_at = pl.ds(pl.multiple_of(q * r_rows, r_rows), r_rows)
        rgrad[rows_at, lane] = t_out[h, q, st_rows : st_rows + r_rows].astype(F32) * scale

    for h in range(2):

        @pl.when(core == h)
        def _():
            loop(0, planes, lambda q: finish_place(h, q))

    loop(0, planes, lambda k: t_cross(k).wait_recv())
    for h in range(2):

        @pl.when(core != h)
        def _():
            loop(0, planes, lambda q: finish_place(h, q))

    e_cross.wait_recv()
    for h in range(2):
        for z_at in range(nz):
            egrad[z_at * e_rows : (z_at + 1) * e_rows, h * lanes : (h + 1) * lanes] = e_out[h, z_at].astype(F32) * scale

    @pl.when(y < 3)
    def _():
        halo_row.wait_send()

    @pl.when(y > 0)
    def _():
        halo_grad.wait_send()

    def finish_y(k):
        weight_y(k).wait_send()
        cot_y(k).wait_send()
        out_y(k).wait()

    loop(1, 4, finish_y)
    for k in range(1, 4):
        loop(1, nx, lambda j: weight_x(k, j).wait_send())
        weight_core(k).wait_send()
    for copy in (e_core, s_core, r_core, e_cross):
        copy.wait_send()
    loop(1, nx, lambda k: e_x(k).wait_send())

    def finish_plane(k):
        e_plane(k).wait_send()
        plane_sum(s_p, s_rp, 1, k).wait_send()
        plane_sum(r_p, r_rp, 2, k).wait_send()
        t_spread(k).wait_send()

    loop(1, planes, finish_plane)

    def finish_z(k):
        z_sum(e_p, e_rp, 0, k).wait_send()
        z_sum(t_z, t_rz, 2, k).wait_send()
        z_spread(t_f, t_g, 4, k).wait_send()

    loop(1, nz, finish_z)
    loop(0, planes, lambda k: t_cross(k).wait_send())


def body(nx, nz, images, reduce_weight, spatial_weight, expand_weight, cotangent):
    image = images[0]
    rows, cols, chans = image.shape
    mid = reduce_weight.shape[1]
    stack_ch, filt = expand_weight.shape
    half_rows, half_cols = rows // 2, cols // 2
    pix = half_rows * half_cols
    planes = nx * 4
    lanes = 128
    e_rows = stack_ch // nz
    f_rows = e_rows // nx
    s_rows = 9 * mid // planes
    r_rows = chans // planes
    t_rows = -(-(s_rows + r_rows) // (8 * nz)) * 8 * nz
    cot_blocks = cotangent[0].reshape(4, pix, filt)
    weights = spatial_weight.reshape(3, 3 * mid, mid)
    vmem = pl.BlockSpec(memory_space=pltpu.VMEM)
    V = pltpu.VMEM
    D = pltpu.SemaphoreType.DMA
    scratch = [
        V(image.shape, BF16),
        V(reduce_weight.shape, BF16),
        V(weights.shape, BF16),
        V((4, pix, filt), F32),
        V((4, stack_ch, filt), BF16),
        V((4, pix, filt), BF16),
        V((2, half_rows + 1, half_cols, 3 * mid), BF16),
        V((rows, cols, mid), F32),
        V((mid // lanes, cols + 16, lanes), F32),
        V((pix, mid), F32),
        V((half_rows, half_cols, stack_ch), BF16),
        V((4, pix, filt), BF16),
        V((pix, stack_ch), F32),
        V((half_rows + 1, half_cols, mid), BF16),
        V((half_rows + 1, half_cols, mid), BF16),
        V((half_cols + 16, mid), F32),
        V((rows, mid // lanes, cols, lanes), F32),
        V((rows, cols, mid), BF16),
        V((chans, mid), F32),
        V((chans // lanes, cols, lanes), F32),
        V((2, nz, 4, e_rows, lanes), BF16),
        V((nz, 4, e_rows, lanes), BF16),
        V((nz, 4, e_rows, lanes), BF16),
        V((nz, 4, e_rows, lanes), BF16),
        V((4, nx, f_rows, lanes), F32),
        V((planes, f_rows, lanes), F32),
        V((f_rows, lanes), F32),
        V((nx, f_rows, lanes), F32),
        V((2, nz, e_rows, lanes), BF16),
        V((2, planes, s_rows, lanes), BF16),
        V((planes, s_rows, lanes), BF16),
        V((planes, s_rows, lanes), BF16),
        V((planes, s_rows, lanes), BF16),
        V((2, planes, r_rows, lanes), BF16),
        V((planes, r_rows, lanes), BF16),
        V((planes, r_rows, lanes), BF16),
        V((planes, r_rows, lanes), BF16),
        V((nz, t_rows // nz, lanes), F32),
        V((nz, t_rows // nz, lanes), F32),
        V((t_rows // nz, lanes), F32),
        V((nz, t_rows // nz, lanes), F32),
        V((2, planes, t_rows, lanes), BF16),
        D((14,)),
        D((14,)),
        D((5 * planes,)),
        D((5 * planes,)),
        D((5 * nz,)),
        D((5 * nz,)),
        D((8 + planes,)),
        D((8 + planes,)),
        D((4 * nx,)),
        D((4 * nx,)),
        D((rows + 4,)),
    ]
    output, input_grad, reduce_grad, spatial_grad, expand_grad = pl.pallas_call(
        functools.partial(block_kernel, nx, nz),
        out_shape=(
            pltpu.VMEM((4, pix, filt), BF16),
            pltpu.VMEM(image.shape, BF16),
            pltpu.VMEM((chans, mid), F32),
            pltpu.VMEM((3, 3 * mid, mid), F32),
            pltpu.VMEM((stack_ch, filt), F32),
        ),
        in_specs=[pl.BlockSpec(memory_space=pltpu.HBM)] * 5,
        out_specs=[vmem] * 5,
        scratch_shapes=scratch,
        compiler_params=pltpu.CompilerParams(
            collective_id=0, has_side_effects=True, vmem_limit_bytes=48 * 1024 * 1024
        ),
    )(image, reduce_weight, weights, expand_weight, cot_blocks)
    return (
        output.reshape((1, 4 * half_rows, half_cols, filt)),
        input_grad[None],
        reduce_grad,
        spatial_grad.reshape(3, 3, mid, mid),
        expand_grad,
    )


def solution(mesh):
    nx = 4 if mesh.shape["dp"] >= 32 else 2
    nz = mesh.shape["dp"] // (2 * nx)
    return jax.shard_map(
        functools.partial(body, nx, nz),
        mesh=mesh,
        in_specs=(
            P("dp", ("space", "chan"), None, None),
            P(),
            P(),
            P(None, ("space", "chan")),
            P("dp", None, None, ("space", "chan")),
        ),
        out_specs=(
            P("dp", None, None, ("space", "chan")),
            P("dp", ("space", "chan"), None, None),
            P(),
            P(),
            P(None, ("space", "chan")),
        ),
        check_vma=False,
    )
```

```python
import functools
import math

import jax
import jax.numpy as jnp
from jax import lax
from jax.experimental import pallas as pl
from jax.experimental.pallas import tpu as pltpu
from jax.sharding import PartitionSpec as P

MESH = pl.DeviceIdType.MESH
F32 = jnp.float32
BF16 = jnp.bfloat16


def sigmoid(pre):
    return 1.0 / (1.0 + jnp.exp(-pre))


def slope_of(pre, sig):
    return sig * (1.0 + pre * (1.0 - sig))


def dot(left, right):
    return jnp.dot(left, right, preferred_element_type=F32)


def dot_tn(left, right):
    return lax.dot_general(left, right, (((0,), (0,)), ((), ())), preferred_element_type=F32)


def dot_nt(left, right):
    return lax.dot_general(left, right, (((1,), (1,)), ((), ())), preferred_element_type=F32)


def loop(low, high, step_fn):
    def step(index, carry):
        step_fn(index)
        return carry

    lax.fori_loop(low, high, step, 0)


def block_kernel(
    nx, nz, img_hbm, wr_hbm, ws_hbm, we, cot,
    out, igrad, rgrad, sgrad, egrad,
    img, wr, ws, slp, wg, cotr, a_s, pre_s, rowbuf, spre_s, stk, obuf, stg, sgp, sgq, sbuf, rg_s, rgp_s, rterm, widebuf,
    e_send, e_rc, e_p, e_rp, e_z, e_rz, e_f, e_g, e_out,
    s_send, s_rc, s_p, s_a1, s_am, s_a2, s_b1, s_bm, s_b2, r_send, r_rc, r_p, r_rp, t_z, t_rz, t_f, t_g, t_out,
    y_send_sem, y_recv_sem, p_send_sem, p_recv_sem, z_send_sem, z_recv_sem, c_send_sem, c_recv_sem, w_send_sem, w_recv_sem, e_send_sem, e_recv_sem, q_send_sem, q_recv_sem, load_sem,
):
    rows, cols, chans = img.shape
    half_cols = cols // 2
    half_rows = rows // 2
    mid = wr.shape[1]
    stack_ch, filt = we.shape
    pix = half_rows * half_cols
    lanes = 128
    planes = nx * 4
    dp = lax.axis_index("dp")
    y = lax.axis_index("space") * 2 + lax.axis_index("chan")
    core = dp % 2
    x = (dp // 2) % nx
    z = dp // (2 * nx)
    plane = x * 4 + y
    scale = 1.0 / math.sqrt(lax.axis_size("dp") * cot.shape[0] * pix)

    def device(z_at, x_at, core_at, y_at):
        return ((z_at * nx + x_at) * 2 + core_at, y_at // 2, y_at % 2)

    def at_y(y_at):
        return device(z, x, core, y_at)

    def at_x(x_at):
        return device(z, x_at, core, y)

    def at_z(z_at):
        return device(z_at, x, core, y)

    def at_plane(place):
        return device(z, place // 4, core, place % 4)

    other_core = device(z, x, 1 - core, y)

    def remote(src, dst, send_sem, recv_sem, target):
        return pltpu.make_async_remote_copy(
            src_ref=src, dst_ref=dst, send_sem=send_sem, recv_sem=recv_sem, device_id=target, device_id_type=MESH
        )

    barrier = pltpu.get_barrier_semaphore()
    pl.semaphore_signal(barrier, inc=1, device_id=other_core, device_id_type=MESH)

    def greet_plane(k):
        pl.semaphore_signal(barrier, inc=1, device_id=at_plane((plane + k) % planes), device_id_type=MESH)

    def greet_z(k):
        pl.semaphore_signal(barrier, inc=1, device_id=at_z((z + k) % nz), device_id_type=MESH)

    loop(1, planes, greet_plane)
    loop(1, nz, greet_z)

    load_wr = pltpu.make_async_copy(wr_hbm, wr, load_sem.at[rows])
    load_ws = pltpu.make_async_copy(ws_hbm, ws, load_sem.at[rows + 1])
    load_we = pltpu.make_async_copy(we, wg.at[0], load_sem.at[rows + 2])
    load_cot = pltpu.make_async_copy(cot.at[y], cotr.at[0], load_sem.at[rows + 3])

    def load_row(p):
        return pltpu.make_async_copy(img_hbm.at[p], img.at[p], load_sem.at[p])

    load_wr.start()
    loop(0, rows, lambda p: load_row(p).start())
    load_ws.start()
    load_we.start()
    load_cot.start()

    rowbuf[:, 0:8] = jnp.zeros((mid // lanes, 8, lanes), F32)

    def reduce_row(p):
        load_row(p).wait()
        pre = dot(img[p], wr[...])
        pre_s[p] = pre
        reduced = pre * sigmoid(pre)
        a_par, a_idx = (p + 1) % 2, (p + 1) // 2
        for block in range(mid // lanes):
            rowbuf[block, 8 : 8 + cols] = reduced[:, block * lanes : (block + 1) * lanes]
            for part, start in enumerate((7, 8, 9)):
                lane = part * mid + block * lanes
                a_s[a_par, a_idx, :, lane : lane + lanes] = rowbuf[block, pl.ds(start, half_cols, stride=2), :].astype(BF16)

    load_wr.wait()
    loop(0, rows, reduce_row)
    pl.semaphore_wait(barrier, planes + nz - 1)

    part_rows = stack_ch // (2 * nx)
    part = pl.ds(pl.multiple_of((core * nx + x) * part_rows, part_rows), part_rows)
    half_part = pl.ds(pl.multiple_of(core * (stack_ch // 2), stack_ch // 2), stack_ch // 2)

    def weight_y(k):
        return remote(we.at[part], wg.at[k, part], y_send_sem.at[k], y_recv_sem.at[k], at_y((y + k) % 4))

    def weight_x(k, j):
        slot = k * nx + j
        return remote(wg.at[k, part], wg.at[k, part], w_send_sem.at[slot], w_recv_sem.at[slot], at_x((x + j) % nx))

    def weight_core(k):
        return remote(wg.at[k, half_part], wg.at[k, half_part], c_send_sem.at[k], c_recv_sem.at[k], other_core)

    def cot_y(k):
        return remote(
            cot.at[(y + k) % 4], cotr.at[k], y_send_sem.at[4 + k], y_recv_sem.at[4 + k], at_y((y + k) % 4)
        )

    def halo_part(index):
        return a_s.at[0, index, :, mid : 3 * mid]

    halo_row = remote(
        halo_part(half_rows), halo_part(0), y_send_sem.at[12], y_recv_sem.at[12], at_y((y + 1) % 4)
    )
    for k in (1, 3, 2):
        weight_y(k).start()

    @pl.when(y < 3)
    def _():
        halo_row.start()

    for k in (1, 3, 2):
        cot_y(k).start()

    take = (
        lax.broadcasted_iota(jnp.int32, (half_cols, cols), 1)
        == 2 * lax.broadcasted_iota(jnp.int32, (half_cols, cols), 0)
    ).astype(F32).astype(BF16)

    def pick_even(i):
        stk[i, :, mid : mid + chans] = dot(take, img[2 * i]).astype(BF16)

    loop(0, half_rows, pick_even)

    def windows(r):
        return a_s[r % 2, r // 2 : r // 2 + half_rows].reshape(pix, 3 * mid)

    load_ws.wait()
    spre_s[...] = dot(windows(1), ws[1]) + dot(windows(2), ws[2])
    for k in (1, 3, 2):
        weight_y(k).wait_recv()
        loop(1, nx, lambda j: weight_x(k, j).start())

    @pl.when(y > 0)
    def _():
        halo_row.wait_recv()
        sbuf[0:8] = jnp.zeros((8, mid), F32)
        sbuf[8 : 8 + half_cols] = a_s[0, 0, :, 2 * mid : 3 * mid].astype(F32)
        a_s[0, 0, :, 0:mid] = sbuf[7 : 7 + half_cols].astype(BF16)

    @pl.when(y == 0)
    def _():
        a_s[0, 0] = jnp.zeros_like(a_s[0, 0])

    spre = spre_s[...] + dot(windows(0), ws[0])
    spre_s[...] = spre
    stk[:, :, 0:mid] = (spre * sigmoid(spre)).astype(BF16).reshape(half_rows, half_cols, mid)

    def out_y(k):
        return remote(
            obuf.at[k], out.at[y], y_send_sem.at[8 + k], y_recv_sem.at[8 + k], at_y((y + 4 - k) % 4)
        )

    def expand_block(k):
        pre = dot(stk[...].reshape(pix, stack_ch), wg[k])
        sig = sigmoid(pre)
        value = (pre * sig).astype(BF16)
        slp[k] = slope_of(pre, sig)
        if k == 0:
            out[y] = value
        else:
            obuf[k] = value

    def weight_relay(k):
        loop(1, nx, lambda j: weight_x(k, j).wait_recv())
        weight_core(k).start()

    e_rows = stack_ch // nz

    def expand_back(k):
        owner = (y + 4 - k) % 4
        grad = (cotr[k].astype(F32) * slp[k]).astype(BF16)
        term = dot_tn(stk[...].reshape(pix, stack_ch), grad).astype(BF16)
        for h in range(2):
            for z_at in range(nz):
                e_send[h, owner, z_at] = term[z_at * e_rows : (z_at + 1) * e_rows, h * lanes : (h + 1) * lanes]
        back = dot_nt(grad, wg[k])
        if k == 0:
            stg[...] = back
        else:
            stg[...] += back

    def e_owner(k):
        return (y + 4 - k) % 4

    def e_core(k):
        owner = e_owner(k)
        return remote(e_send.at[1 - core, owner], e_rc.at[owner], c_send_sem.at[4 + k], c_recv_sem.at[4 + k], other_core)

    def e_sum(k, j):
        owner, z_at, slot = e_owner(k), (z + j) % nz, k * nz + j
        return remote(
            e_p.at[owner, z_at], e_rp.at[owner, j], e_send_sem.at[slot], e_recv_sem.at[slot], at_z(z_at)
        )

    def e_relay(k):
        owner = e_owner(k)
        e_core(k).wait_recv()

        def one(z_at):
            e_p[owner, z_at] = (e_send[core, owner, z_at].astype(F32) + e_rc[owner, z_at].astype(F32)).astype(BF16)

        loop(0, nz, one)
        loop(1, nz, lambda j: e_sum(k, j).start())

    load_we.wait()
    load_cot.wait()
    expand_block(0)
    weight_relay(1)
    expand_back(0)
    e_core(0).start()
    weight_relay(3)
    weight_core(1).wait_recv()
    expand_block(1)
    weight_relay(2)
    e_relay(0)
    weight_core(3).wait_recv()
    expand_block(3)
    cot_y(1).wait_recv()
    expand_back(1)
    e_core(1).start()
    weight_core(2).wait_recv()
    expand_block(2)
    e_relay(1)
    cot_y(3).wait_recv()
    expand_back(3)
    e_core(3).start()
    cot_y(2).wait_recv()
    out_y(1).start()
    out_y(3).start()
    expand_back(2)
    e_core(2).start()

    def core_sum(send, got, k):
        return remote(send.at[1 - core], got, c_send_sem.at[k], c_recv_sem.at[k], other_core)

    def plane_sum(summed, got, group, k):
        slot = group * planes + k
        place = (plane + k) % planes
        return remote(
            summed.at[place], got.at[k], p_send_sem.at[slot], p_recv_sem.at[slot], at_plane(place)
        )

    def add_core(send, got, summed):
        def one(q):
            summed[q] = (send[core, q].astype(F32) + got[q].astype(F32)).astype(BF16)

        loop(0, summed.shape[0], one)

    def plane_total(summed, got, group):
        def one(k, total):
            plane_sum(summed, got, group, k).wait_recv()
            return total + got[k].astype(F32)

        return lax.fori_loop(1, planes, one, summed[plane].astype(F32))

    def z_sum(src, dst, group, k):
        slot = group * nz + k
        return remote(
            src.at[(z + k) % nz], dst.at[k], z_send_sem.at[slot], z_recv_sem.at[slot], at_z((z + k) % nz)
        )

    def z_spread(src, dst, group, k):
        slot = group * nz + k
        return remote(src, dst.at[z], z_send_sem.at[slot], z_recv_sem.at[slot], at_z((z + k) % nz))

    def z_total(src, dst, group):
        def one(k, total):
            z_sum(src, dst, group, k).wait_recv()
            return total + dst[k].astype(F32)

        return lax.fori_loop(1, nz, one, src[z].astype(F32))

    spre = spre_s[...]
    sig = sigmoid(spre)
    sgrad_pre = stg[:, 0:mid] * slope_of(spre, sig)
    sgp[0:half_rows] = sgrad_pre.astype(BF16).reshape(half_rows, half_cols, mid)
    halo_grad = remote(sgp.at[0], sgp.at[half_rows], y_send_sem.at[13], y_recv_sem.at[13], at_y((y + 3) % 4))

    @pl.when(y > 0)
    def _():
        halo_grad.start()

    s_rows = mid * 3 // planes
    flat = sgp[0:half_rows].reshape(pix, mid)

    def s_core(r):
        at = slice(r * s_rows, (r + 1) * s_rows)
        return remote(
            s_send.at[1 - core, :, :, at], s_rc.at[:, :, at], e_send_sem.at[r * nz], e_recv_sem.at[r * nz], other_core
        )

    for r in range(3):
        term = dot_tn(windows(r), flat).astype(BF16)
        for h in range(2):
            for q in range(planes):
                s_send[h, q // 4, q % 4, r * s_rows : (r + 1) * s_rows] = term[
                    q * s_rows : (q + 1) * s_rows, h * lanes : (h + 1) * lanes
                ]
        s_core(r).start()
    e_relay(3)

    def add_spatial(at):
        def one(q):
            x_at, y_at = q // 4, q % 4
            s_p[x_at, y_at, at] = (s_send[core, x_at, y_at, at].astype(F32) + s_rc[x_at, y_at, at].astype(F32)).astype(BF16)

        loop(0, planes, one)

    a_rows, b_rows = 2 * s_rows, s_rows

    def over_x(src, dst, group, k):
        slot = 4 * group + k
        return remote(src, dst, q_send_sem.at[slot], q_recv_sem.at[slot], at_x((x + k) % nx))

    def over_y(src, dst, group, k):
        slot = 4 * group + k
        return remote(src, dst, q_send_sem.at[slot], q_recv_sem.at[slot], at_y((y + k) % 4))

    def s_a_first(k):
        return over_x(s_p.at[(x + k) % nx, :, 0:a_rows], s_a1.at[k], 0, k)

    def s_b_first(k):
        return over_y(s_p.at[:, (y + k) % 4, a_rows : a_rows + b_rows], s_b1.at[k], 1, k)

    def s_a_second(k):
        return over_y(s_am.at[(y + k) % 4], s_a2.at[k], 2, k)

    def s_b_second(k):
        return over_x(s_bm.at[(x + k) % nx], s_b2.at[k], 3, k)

    s_core(0).wait_recv()
    s_core(1).wait_recv()
    add_spatial(slice(0, a_rows))
    loop(1, nx, lambda k: s_a_first(k).start())
    s_core(2).wait_recv()
    add_spatial(slice(a_rows, a_rows + b_rows))
    loop(1, 4, lambda k: s_b_first(k).start())
    e_relay(2)

    @pl.when(y < 3)
    def _():
        halo_grad.wait_recv()

    @pl.when(y == 3)
    def _():
        sgp[half_rows] = jnp.zeros_like(sgp[half_rows])

    sbuf[half_cols : half_cols + 8] = jnp.zeros((8, mid), F32)

    def shift_row(i):
        sbuf[0:half_cols] = sgp[i].astype(F32)
        sgq[i] = sbuf[1 : 1 + half_cols].astype(BF16)

    loop(0, half_rows + 1, shift_row)
    here = sgp[0:half_rows].reshape(pix, mid)
    here_next = sgq[0:half_rows].reshape(pix, mid)

    def weave(row_par, col_par, value):
        value = value.reshape(half_rows, half_cols, mid)
        for i in range(half_rows):
            for block in range(mid // lanes):
                rg_s[2 * i + row_par, block, pl.ds(col_par, half_cols, stride=2), :] = value[
                    i, :, block * lanes : (block + 1) * lanes
                ]

    def tap(r, c):
        return ws[r, c * mid : (c + 1) * mid, :]

    weave(0, 0, dot_nt(here, tap(1, 1)))
    weave(0, 1, dot_nt(here, tap(1, 2)) + dot_nt(here_next, tap(1, 0)))
    below = sgp[1 : half_rows + 1].reshape(pix, mid)
    below_next = sgq[1 : half_rows + 1].reshape(pix, mid)
    weave(1, 0, dot_nt(here, tap(2, 1)) + dot_nt(below, tap(0, 1)))
    weave(
        1, 1,
        dot_nt(here, tap(2, 2)) + dot_nt(here_next, tap(2, 0)) + dot_nt(below, tap(0, 2)) + dot_nt(below_next, tap(0, 0)),
    )
    rterm[...] = jnp.zeros_like(rterm)

    def reduce_back(p):
        pre = pre_s[p]
        canvas = jnp.concatenate([rg_s[p, block] for block in range(mid // lanes)], axis=1)
        grad = (canvas * slope_of(pre, sigmoid(pre))).astype(BF16)
        rgp_s[p] = grad
        rterm[...] += dot_tn(img[p], grad)

    loop(0, rows, reduce_back)
    r_rows = chans // planes
    for h in range(2):
        for q in range(planes):
            r_send[h, q] = rterm[q * r_rows : (q + 1) * r_rows, h * lanes : (h + 1) * lanes].astype(BF16)
    r_core = core_sum(r_send, r_rc, 9)
    r_core.start()

    def input_row(p):
        wide = dot_nt(rgp_s[p], wr[...])

        @pl.when(p % 2 == 1)
        def _():
            igrad[p] = wide.astype(BF16)

        @pl.when(p % 2 == 0)
        def _():
            first = pl.ds(pl.multiple_of((p // 2) * half_cols, half_cols), half_cols)
            for block in range(chans // lanes):
                lane = slice(block * lanes, (block + 1) * lanes)
                widebuf[block] = wide[:, lane]
                widebuf[block, pl.ds(0, half_cols, stride=2), :] = (
                    widebuf[block, pl.ds(0, half_cols, stride=2), :]
                    + stg[first, mid + block * lanes : mid + (block + 1) * lanes]
                )
                igrad[p, :, lane] = widebuf[block].astype(BF16)

    loop(0, half_rows, input_row)
    r_core.wait_recv()
    add_core(r_send, r_rc, r_p)
    loop(1, planes, lambda k: plane_sum(r_p, r_rp, 2, k).start())

    loop(1, nx, lambda k: s_a_first(k).wait_recv())
    for y_at in range(4):
        total = s_p[x, y_at, 0:a_rows].astype(F32)
        for k in range(1, nx):
            total = total + s_a1[k, y_at].astype(F32)
        s_am[y_at] = total.astype(BF16)
    loop(1, 4, lambda k: s_a_second(k).start())
    loop(1, 4, lambda k: s_b_first(k).wait_recv())
    for x_at in range(nx):
        total = s_p[x_at, y, a_rows : a_rows + b_rows].astype(F32)
        for k in range(1, 4):
            total = total + s_b1[k, x_at].astype(F32)
        s_bm[x_at] = total.astype(BF16)
    loop(1, nx, lambda k: s_b_second(k).start())
    loop(half_rows, rows, input_row)

    st_rows, rt_rows, t_rows = 3 * s_rows, r_rows, t_z.shape[0] * t_z.shape[1]
    total_a = s_am[y].astype(F32)
    for k in range(1, 4):
        s_a_second(k).wait_recv()
        total_a = total_a + s_a2[k].astype(F32)
    total_b = s_bm[x].astype(F32)
    for k in range(1, nx):
        s_b_second(k).wait_recv()
        total_b = total_b + s_b2[k].astype(F32)
    total = [total_a, total_b, plane_total(r_p, r_rp, 2)]
    if t_rows > st_rows + rt_rows:
        total.append(jnp.zeros((t_rows - st_rows - rt_rows, lanes), F32))
    t_z[...] = jnp.concatenate(total, axis=0).reshape(t_z.shape)
    loop(1, nz, lambda k: z_sum(t_z, t_rz, 2, k).start())

    out_y(2).start()

    for k in range(4):
        owner = e_owner(k)

        def e_add(j, total):
            e_sum(k, j).wait_recv()
            return total + e_rp[owner, j].astype(F32)

        e_z[owner] = lax.fori_loop(1, nz, e_add, e_p[owner, z].astype(F32)).reshape(e_z.shape[1:])

    def e_plane(k):
        place = (plane + k) % planes
        return remote(
            e_z.at[place % 4, place // 4], e_rz.at[k], p_send_sem.at[k], p_recv_sem.at[k], at_plane(place)
        )

    loop(1, planes, lambda k: e_plane(k).start())

    t_f[...] = z_total(t_z, t_rz, 2)
    loop(1, nz, lambda k: z_spread(t_f, t_g, 4, k).start())

    def e_total(k, total):
        e_plane(k).wait_recv()
        return total + e_rz[k]

    e_f[...] = lax.fori_loop(1, planes, e_total, e_z[y, x])

    def e_x(k):
        return remote(
            e_f, e_g.at[x], p_send_sem.at[3 * planes + k], p_recv_sem.at[3 * planes + k], at_x((x + k) % nx)
        )

    loop(1, nx, lambda k: e_x(k).start())

    @pl.when(y < 3)
    def _():
        halo_row.wait_send()

    @pl.when(y > 0)
    def _():
        halo_grad.wait_send()

    for k in range(1, 4):
        weight_y(k).wait_send()
        cot_y(k).wait_send()
        loop(1, nx, lambda j: weight_x(k, j).wait_send())
        weight_core(k).wait_send()
    for k in range(4):
        e_core(k).wait_send()
        loop(1, nz, lambda j: e_sum(k, j).wait_send())
    for r in range(3):
        s_core(r).wait_send()
    r_core.wait_send()
    loop(1, planes, lambda k: plane_sum(r_p, r_rp, 2, k).wait_send())
    for k in range(1, 4):
        if k < nx:
            s_a_first(k).wait_send()
            s_b_second(k).wait_send()
        s_b_first(k).wait_send()
        s_a_second(k).wait_send()

    loop(1, nz, lambda k: z_spread(t_f, t_g, 4, k).wait_recv())
    t_g[z] = t_f[...]
    t_out[core, x, y] = t_g[...].reshape(t_rows, lanes).astype(BF16)

    part_a, part_b = slice(0, a_rows), slice(a_rows, t_rows)

    def t_a_first(k):
        return over_y(t_out.at[core, x, y, part_a], t_out.at[core, x, y, part_a], 4, k)

    def t_b_first(k):
        return over_x(t_out.at[core, x, y, part_b], t_out.at[core, x, y, part_b], 5, k)

    def t_a_second(k):
        return over_x(t_out.at[core, x, :, part_a], t_out.at[core, x, :, part_a], 6, k)

    def t_b_second(k):
        return over_y(t_out.at[core, :, y, part_b], t_out.at[core, :, y, part_b], 7, k)

    def t_a_cross(k):
        at = t_out.at[core, (x + nx - k) % nx, :, part_a]
        return remote(at, at, c_send_sem.at[11 + k], c_recv_sem.at[11 + k], other_core)

    def t_b_cross(k):
        at = t_out.at[core, :, (y + 4 - k) % 4, part_b]
        return remote(at, at, c_send_sem.at[15 + k], c_recv_sem.at[15 + k], other_core)

    loop(1, 4, lambda k: t_a_first(k).start())
    loop(1, nx, lambda k: t_b_first(k).start())

    loop(1, 4, lambda k: t_a_first(k).wait_recv())
    loop(1, nx, lambda k: t_a_second(k).start())
    loop(1, nx, lambda k: t_b_first(k).wait_recv())
    loop(1, 4, lambda k: t_b_second(k).start())
    t_a_cross(0).start()
    t_b_cross(0).start()
    loop(1, nx, lambda k: e_x(k).wait_recv())
    e_g[x] = e_f[...]
    e_out[core, z] = e_g[...].reshape(e_rows, lanes).astype(BF16)

    def e_back(k):
        slot = nz + k
        return remote(
            e_out.at[core, z], e_out.at[core, z], z_send_sem.at[slot], z_recv_sem.at[slot], at_z((z + k) % nz)
        )

    loop(1, nz, lambda k: e_back(k).start())

    for k in (1, 3, 2):
        if k < nx:
            t_a_second(k).wait_recv()
            t_a_cross(k).start()
        t_b_second(k).wait_recv()
        t_b_cross(k).start()
    loop(1, nz, lambda k: e_back(k).wait())
    e_cross = remote(e_out.at[core], e_out.at[core], c_send_sem.at[10], c_recv_sem.at[10], other_core)
    e_cross.start()

    def finish_place(h, q):
        lane = slice(h * lanes, (h + 1) * lanes)
        for r in range(3):
            rows_at = pl.ds(pl.multiple_of(q * s_rows, s_rows), s_rows)
            sgrad[r, rows_at, lane] = t_out[h, q // 4, q % 4, r * s_rows : (r + 1) * s_rows].astype(F32) * scale
        rows_at = pl.ds(pl.multiple_of(q * r_rows, r_rows), r_rows)
        rgrad[rows_at, lane] = t_out[h, q // 4, q % 4, st_rows : st_rows + r_rows].astype(F32) * scale

    for h in range(2):

        @pl.when(core == h)
        def _():
            loop(0, planes, lambda q: finish_place(h, q))

    loop(0, nx, lambda k: t_a_cross(k).wait_recv())
    loop(0, 4, lambda k: t_b_cross(k).wait_recv())
    for h in range(2):

        @pl.when(core != h)
        def _():
            loop(0, planes, lambda q: finish_place(h, q))

    e_cross.wait_recv()
    for h in range(2):
        for z_at in range(nz):
            egrad[z_at * e_rows : (z_at + 1) * e_rows, h * lanes : (h + 1) * lanes] = e_out[h, z_at].astype(F32) * scale

    for k in range(1, 4):
        out_y(k).wait()
        t_a_first(k).wait_send()
        t_b_second(k).wait_send()
        t_b_cross(k).wait_send()
        if k < nx:
            e_x(k).wait_send()
            t_b_first(k).wait_send()
            t_a_second(k).wait_send()
            t_a_cross(k).wait_send()
    t_a_cross(0).wait_send()
    t_b_cross(0).wait_send()
    e_cross.wait_send()
    loop(1, planes, lambda k: e_plane(k).wait_send())

    def finish_z(k):
        z_sum(t_z, t_rz, 2, k).wait_send()
        z_spread(t_f, t_g, 4, k).wait_send()

    loop(1, nz, finish_z)


def place_kernel(cuts, *refs):
    count = len(cuts)
    sources, targets, sem = refs[:count], refs[count : 2 * count], refs[2 * count]
    copies = []
    for source, target, pieces in zip(sources, targets, cuts):
        size = source.shape[0] // pieces
        for piece in range(pieces):
            at = pl.ds(piece * size, size)
            copies.append(pltpu.make_async_copy(source.at[at], target.at[at], sem.at[len(copies)]))
    for copy in copies:
        copy.start()
    for copy in copies:
        copy.wait()


def body(nx, nz, images, reduce_weight, spatial_weight, expand_weight, cotangent):
    image = images[0]
    rows, cols, chans = image.shape
    mid = reduce_weight.shape[1]
    stack_ch, filt = expand_weight.shape
    half_rows, half_cols = rows // 2, cols // 2
    pix = half_rows * half_cols
    planes = nx * 4
    lanes = 128
    e_rows = stack_ch // nz
    f_rows = e_rows // nx
    s_rows = 9 * mid // planes
    a_rows, b_rows = s_rows // 3 * 2, s_rows // 3
    r_rows = chans // planes
    t_rows = -(-(s_rows + r_rows) // (8 * nz)) * 8 * nz
    cot_blocks = cotangent[0].reshape(4, pix, filt)
    weights = spatial_weight.reshape(3, 3 * mid, mid)
    vmem = pl.BlockSpec(memory_space=pltpu.VMEM)
    V = pltpu.VMEM
    D = pltpu.SemaphoreType.DMA
    scratch = [
        V(image.shape, BF16),
        V(reduce_weight.shape, BF16),
        V(weights.shape, BF16),
        V((4, pix, filt), F32),
        V((4, stack_ch, filt), BF16),
        V((4, pix, filt), BF16),
        V((2, half_rows + 1, half_cols, 3 * mid), BF16),
        V((rows, cols, mid), F32),
        V((mid // lanes, cols + 16, lanes), F32),
        V((pix, mid), F32),
        V((half_rows, half_cols, stack_ch), BF16),
        V((4, pix, filt), BF16),
        V((pix, stack_ch), F32),
        V((half_rows + 1, half_cols, mid), BF16),
        V((half_rows + 1, half_cols, mid), BF16),
        V((half_cols + 16, mid), F32),
        V((rows, mid // lanes, cols, lanes), F32),
        V((rows, cols, mid), BF16),
        V((chans, mid), F32),
        V((chans // lanes, cols, lanes), F32),
        V((2, 4, nz, e_rows, lanes), BF16),
        V((4, nz, e_rows, lanes), BF16),
        V((4, nz, e_rows, lanes), BF16),
        V((4, nz, e_rows, lanes), BF16),
        V((4, nx, f_rows, lanes), F32),
        V((planes, f_rows, lanes), F32),
        V((f_rows, lanes), F32),
        V((nx, f_rows, lanes), F32),
        V((2, nz, e_rows, lanes), BF16),
        V((2, nx, 4, s_rows, lanes), BF16),
        V((nx, 4, s_rows, lanes), BF16),
        V((nx, 4, s_rows, lanes), BF16),
        V((nx, 4, a_rows, lanes), BF16),
        V((4, a_rows, lanes), BF16),
        V((4, a_rows, lanes), BF16),
        V((4, nx, b_rows, lanes), BF16),
        V((nx, b_rows, lanes), BF16),
        V((nx, b_rows, lanes), BF16),
        V((2, planes, r_rows, lanes), BF16),
        V((planes, r_rows, lanes), BF16),
        V((planes, r_rows, lanes), BF16),
        V((planes, r_rows, lanes), BF16),
        V((nz, t_rows // nz, lanes), F32),
        V((nz, t_rows // nz, lanes), F32),
        V((t_rows // nz, lanes), F32),
        V((nz, t_rows // nz, lanes), F32),
        V((2, nx, 4, t_rows, lanes), BF16),
        D((14,)),
        D((14,)),
        D((5 * planes,)),
        D((5 * planes,)),
        D((5 * nz,)),
        D((5 * nz,)),
        D((19,)),
        D((19,)),
        D((4 * nx,)),
        D((4 * nx,)),
        D((4 * nz,)),
        D((4 * nz,)),
        D((32,)),
        D((32,)),
        D((rows + 4,)),
    ]
    results = pl.pallas_call(
        functools.partial(block_kernel, nx, nz),
        out_shape=(
            pltpu.VMEM((4, pix, filt), BF16),
            pltpu.VMEM(image.shape, BF16),
            pltpu.VMEM((chans, mid), F32),
            pltpu.VMEM((3, 3 * mid, mid), F32),
            pltpu.VMEM((stack_ch, filt), F32),
        ),
        in_specs=[pl.BlockSpec(memory_space=pltpu.HBM)] * 5,
        out_specs=[vmem] * 5,
        scratch_shapes=scratch,
        compiler_params=pltpu.CompilerParams(
            collective_id=0, has_side_effects=True, vmem_limit_bytes=48 * 1024 * 1024
        ),
    )(image, reduce_weight, weights, expand_weight, cot_blocks)
    cuts = (2, 4, 1, 3, 2)
    output, input_grad, reduce_grad, spatial_grad, expand_grad = pl.pallas_call(
        functools.partial(place_kernel, cuts),
        out_shape=[jax.ShapeDtypeStruct(result.shape, result.dtype) for result in results],
        in_specs=[pl.BlockSpec(memory_space=pl.ANY)] * 5,
        out_specs=[pl.BlockSpec(memory_space=pl.ANY)] * 5,
        scratch_shapes=[D((sum(cuts),))],
        compiler_params=pltpu.CompilerParams(vmem_limit_bytes=2 * 1024 * 1024),
    )(*results)
    return (
        output.reshape((1, 4 * half_rows, half_cols, filt)),
        input_grad[None],
        reduce_grad,
        spatial_grad.reshape(3, 3, mid, mid),
        expand_grad,
    )


def solution(mesh):
    nx = 4 if mesh.shape["dp"] >= 32 else 2
    nz = mesh.shape["dp"] // (2 * nx)
    return jax.shard_map(
        functools.partial(body, nx, nz),
        mesh=mesh,
        in_specs=(
            P("dp", ("space", "chan"), None, None),
            P(),
            P(),
            P(None, ("space", "chan")),
            P("dp", None, None, ("space", "chan")),
        ),
        out_specs=(
            P("dp", None, None, ("space", "chan")),
            P("dp", ("space", "chan"), None, None),
            P(),
            P(),
            P(None, ("space", "chan")),
        ),
        check_vma=False,
    )
```

```python
import functools
import math

import jax
import jax.numpy as jnp
from jax import lax
from jax.experimental import pallas as pl
from jax.experimental.pallas import tpu as pltpu
from jax.sharding import PartitionSpec as P

MESH = pl.DeviceIdType.MESH
F32 = jnp.float32
BF16 = jnp.bfloat16


def sigmoid(pre):
    return 1.0 / (1.0 + jnp.exp(-pre))


def slope_of(pre, sig):
    return sig * (1.0 + pre * (1.0 - sig))


def dot(left, right):
    return jnp.dot(left, right, preferred_element_type=F32)


def dot_tn(left, right):
    return lax.dot_general(left, right, (((0,), (0,)), ((), ())), preferred_element_type=F32)


def dot_nt(left, right):
    return lax.dot_general(left, right, (((1,), (1,)), ((), ())), preferred_element_type=F32)


def loop(low, high, step_fn):
    def step(index, carry):
        step_fn(index)
        return carry

    lax.fori_loop(low, high, step, 0)


def block_kernel(
    nx, nz, img_hbm, wr_hbm, ws_hbm, we, cot,
    out, igrad, rgrad, sgrad, egrad,
    img, wr, ws, slp, wg, cotr, a_s, pre_s, rowbuf, spre_s, stk, obuf, stg, sgp, sgq, sbuf, rg_s, rgp_s, rterm, widebuf,
    e_send, e_rc, e_p, e_rp, e_z, e_rz, e_f, e_g, e_out,
    s_send, s_rc, s_p, s_a1, s_am, s_a2, s_b1, s_bm, s_b2, r_send, r_rc, r_p, r_rp, t_z, t_rz, t_f, t_g, t_out,
    y_send_sem, y_recv_sem, p_send_sem, p_recv_sem, z_send_sem, z_recv_sem, c_send_sem, c_recv_sem, w_send_sem, w_recv_sem, e_send_sem, e_recv_sem, q_send_sem, q_recv_sem, load_sem,
):
    rows, cols, chans = img.shape
    half_cols = cols // 2
    half_rows = rows // 2
    mid = wr.shape[1]
    stack_ch, filt = we.shape
    pix = half_rows * half_cols
    lanes = 128
    planes = nx * 4
    dp = lax.axis_index("dp")
    y = lax.axis_index("space") * 2 + lax.axis_index("chan")
    core = dp % 2
    x = (dp // 2) % nx
    z = dp // (2 * nx)
    plane = x * 4 + y
    scale = 1.0 / math.sqrt(lax.axis_size("dp") * cot.shape[0] * pix)

    def device(z_at, x_at, core_at, y_at):
        return ((z_at * nx + x_at) * 2 + core_at, y_at // 2, y_at % 2)

    def at_y(y_at):
        return device(z, x, core, y_at)

    def at_x(x_at):
        return device(z, x_at, core, y)

    def at_z(z_at):
        return device(z_at, x, core, y)

    def at_plane(place):
        return device(z, place // 4, core, place % 4)

    other_core = device(z, x, 1 - core, y)

    def remote(src, dst, send_sem, recv_sem, target):
        return pltpu.make_async_remote_copy(
            src_ref=src, dst_ref=dst, send_sem=send_sem, recv_sem=recv_sem, device_id=target, device_id_type=MESH
        )

    barrier = pltpu.get_barrier_semaphore()
    pl.semaphore_signal(barrier, inc=1, device_id=other_core, device_id_type=MESH)

    def greet_plane(k):
        pl.semaphore_signal(barrier, inc=1, device_id=at_plane((plane + k) % planes), device_id_type=MESH)

    def greet_z(k):
        pl.semaphore_signal(barrier, inc=1, device_id=at_z((z + k) % nz), device_id_type=MESH)

    loop(1, planes, greet_plane)
    loop(1, nz, greet_z)

    load_wr = pltpu.make_async_copy(wr_hbm, wr, load_sem.at[rows])
    load_ws = pltpu.make_async_copy(ws_hbm, ws, load_sem.at[rows + 1])
    load_we = pltpu.make_async_copy(we, wg.at[0], load_sem.at[rows + 2])
    load_cot = pltpu.make_async_copy(cot.at[y], cotr.at[0], load_sem.at[rows + 3])

    def load_row(p):
        return pltpu.make_async_copy(img_hbm.at[p], img.at[p], load_sem.at[p])

    load_wr.start()
    loop(0, rows, lambda p: load_row(p).start())
    load_ws.start()
    load_we.start()
    load_cot.start()

    rowbuf[:, 0:8] = jnp.zeros((mid // lanes, 8, lanes), F32)

    def reduce_row(p):
        load_row(p).wait()
        pre = dot(img[p], wr[...])
        pre_s[p] = pre
        reduced = pre * sigmoid(pre)
        a_par, a_idx = (p + 1) % 2, (p + 1) // 2
        for block in range(mid // lanes):
            rowbuf[block, 8 : 8 + cols] = reduced[:, block * lanes : (block + 1) * lanes]
            for part, start in enumerate((7, 8, 9)):
                lane = part * mid + block * lanes
                a_s[a_par, a_idx, :, lane : lane + lanes] = rowbuf[block, pl.ds(start, half_cols, stride=2), :].astype(BF16)

    load_wr.wait()
    loop(0, rows, reduce_row)
    pl.semaphore_wait(barrier, planes + nz - 1)

    part_rows = stack_ch // (2 * nx)
    part = pl.ds(pl.multiple_of((core * nx + x) * part_rows, part_rows), part_rows)
    half_part = pl.ds(pl.multiple_of(core * (stack_ch // 2), stack_ch // 2), stack_ch // 2)

    def weight_y(k):
        return remote(we.at[part], wg.at[k, part], y_send_sem.at[k], y_recv_sem.at[k], at_y((y + k) % 4))

    def weight_x(k, j):
        slot = k * nx + j
        return remote(wg.at[k, part], wg.at[k, part], w_send_sem.at[slot], w_recv_sem.at[slot], at_x((x + j) % nx))

    def weight_core(k):
        return remote(wg.at[k, half_part], wg.at[k, half_part], c_send_sem.at[k], c_recv_sem.at[k], other_core)

    def cot_y(k):
        return remote(
            cot.at[(y + k) % 4], cotr.at[k], y_send_sem.at[4 + k], y_recv_sem.at[4 + k], at_y((y + k) % 4)
        )

    def halo_part(index):
        return a_s.at[0, index, :, mid : 3 * mid]

    halo_row = remote(
        halo_part(half_rows), halo_part(0), y_send_sem.at[12], y_recv_sem.at[12], at_y((y + 1) % 4)
    )
    for k in (1, 3, 2):
        weight_y(k).start()

    @pl.when(y < 3)
    def _():
        halo_row.start()

    for k in (1, 3, 2):
        cot_y(k).start()

    take = (
        lax.broadcasted_iota(jnp.int32, (half_cols, cols), 1)
        == 2 * lax.broadcasted_iota(jnp.int32, (half_cols, cols), 0)
    ).astype(F32).astype(BF16)

    def pick_even(i):
        stk[i, :, mid : mid + chans] = dot(take, img[2 * i]).astype(BF16)

    loop(0, half_rows, pick_even)

    def windows(r):
        return a_s[r % 2, r // 2 : r // 2 + half_rows].reshape(pix, 3 * mid)

    load_ws.wait()
    spre_s[...] = dot(windows(1), ws[1]) + dot(windows(2), ws[2])
    for k in (1, 3, 2):
        weight_y(k).wait_recv()
        loop(1, nx, lambda j: weight_x(k, j).start())

    @pl.when(y > 0)
    def _():
        halo_row.wait_recv()
        sbuf[0:8] = jnp.zeros((8, mid), F32)
        sbuf[8 : 8 + half_cols] = a_s[0, 0, :, 2 * mid : 3 * mid].astype(F32)
        a_s[0, 0, :, 0:mid] = sbuf[7 : 7 + half_cols].astype(BF16)

    @pl.when(y == 0)
    def _():
        a_s[0, 0] = jnp.zeros_like(a_s[0, 0])

    spre = spre_s[...] + dot(windows(0), ws[0])
    spre_s[...] = spre
    stk[:, :, 0:mid] = (spre * sigmoid(spre)).astype(BF16).reshape(half_rows, half_cols, mid)

    def out_y(k):
        return remote(
            obuf.at[k], out.at[y], y_send_sem.at[8 + k], y_recv_sem.at[8 + k], at_y((y + 4 - k) % 4)
        )

    def expand_block(k):
        pre = dot(stk[...].reshape(pix, stack_ch), wg[k])
        sig = sigmoid(pre)
        value = (pre * sig).astype(BF16)
        slp[k] = slope_of(pre, sig)
        if k == 0:
            out[y] = value
        else:
            obuf[k] = value

    def weight_relay(k):
        loop(1, nx, lambda j: weight_x(k, j).wait_recv())
        weight_core(k).start()

    e_rows = stack_ch // nz

    def expand_back(k):
        owner = (y + 4 - k) % 4
        grad = (cotr[k].astype(F32) * slp[k]).astype(BF16)
        term = dot_tn(stk[...].reshape(pix, stack_ch), grad).astype(BF16)
        for h in range(2):
            for z_at in range(nz):
                e_send[h, owner, z_at] = term[z_at * e_rows : (z_at + 1) * e_rows, h * lanes : (h + 1) * lanes]
        back = dot_nt(grad, wg[k])
        if k == 0:
            stg[...] = back
        else:
            stg[...] += back

    def e_owner(k):
        return (y + 4 - k) % 4

    def e_core(k):
        owner = e_owner(k)
        return remote(e_send.at[1 - core, owner], e_rc.at[owner], c_send_sem.at[4 + k], c_recv_sem.at[4 + k], other_core)

    def e_sum(k, j):
        owner, z_at, slot = e_owner(k), (z + j) % nz, k * nz + j
        return remote(
            e_p.at[owner, z_at], e_rp.at[owner, j], e_send_sem.at[slot], e_recv_sem.at[slot], at_z(z_at)
        )

    def e_relay(k):
        owner = e_owner(k)
        e_core(k).wait_recv()

        def one(z_at):
            e_p[owner, z_at] = (e_send[core, owner, z_at].astype(F32) + e_rc[owner, z_at].astype(F32)).astype(BF16)

        loop(0, nz, one)
        loop(1, nz, lambda j: e_sum(k, j).start())

    load_we.wait()
    load_cot.wait()
    expand_block(0)
    weight_relay(1)
    expand_back(0)
    e_core(0).start()
    weight_relay(3)
    weight_core(1).wait_recv()
    expand_block(1)
    weight_relay(2)
    e_relay(0)
    weight_core(3).wait_recv()
    expand_block(3)
    cot_y(1).wait_recv()
    expand_back(1)
    e_core(1).start()
    weight_core(2).wait_recv()
    expand_block(2)
    e_relay(1)
    cot_y(3).wait_recv()
    expand_back(3)
    e_core(3).start()
    cot_y(2).wait_recv()
    out_y(1).start()
    out_y(3).start()
    expand_back(2)
    e_core(2).start()
    e_relay(3)

    def core_sum(send, got, k):
        return remote(send.at[1 - core], got, c_send_sem.at[k], c_recv_sem.at[k], other_core)

    def plane_sum(summed, got, group, k):
        slot = group * planes + k
        place = (plane + k) % planes
        return remote(
            summed.at[place], got.at[k], p_send_sem.at[slot], p_recv_sem.at[slot], at_plane(place)
        )

    def add_core(send, got, summed):
        def one(q):
            summed[q] = (send[core, q].astype(F32) + got[q].astype(F32)).astype(BF16)

        loop(0, summed.shape[0], one)

    def plane_total(summed, got, group):
        def one(k, total):
            plane_sum(summed, got, group, k).wait_recv()
            return total + got[k].astype(F32)

        return lax.fori_loop(1, planes, one, summed[plane].astype(F32))

    def z_sum(src, dst, group, k):
        slot = group * nz + k
        return remote(
            src.at[(z + k) % nz], dst.at[k], z_send_sem.at[slot], z_recv_sem.at[slot], at_z((z + k) % nz)
        )

    def z_spread(src, dst, group, k):
        slot = group * nz + k
        return remote(src, dst.at[z], z_send_sem.at[slot], z_recv_sem.at[slot], at_z((z + k) % nz))

    def z_total(src, dst, group):
        def one(k, total):
            z_sum(src, dst, group, k).wait_recv()
            return total + dst[k].astype(F32)

        return lax.fori_loop(1, nz, one, src[z].astype(F32))

    spre = spre_s[...]
    sig = sigmoid(spre)
    sgrad_pre = stg[:, 0:mid] * slope_of(spre, sig)
    sgp[0:half_rows] = sgrad_pre.astype(BF16).reshape(half_rows, half_cols, mid)
    halo_grad = remote(sgp.at[0], sgp.at[half_rows], y_send_sem.at[13], y_recv_sem.at[13], at_y((y + 3) % 4))

    @pl.when(y > 0)
    def _():
        halo_grad.start()

    s_rows = mid * 3 // planes
    flat = sgp[0:half_rows].reshape(pix, mid)
    for r in range(3):
        term = dot_tn(windows(r), flat).astype(BF16)
        for h in range(2):
            for q in range(planes):
                s_send[h, q // 4, q % 4, r * s_rows : (r + 1) * s_rows] = term[
                    q * s_rows : (q + 1) * s_rows, h * lanes : (h + 1) * lanes
                ]
    s_core = core_sum(s_send, s_rc, 8)
    s_core.start()
    e_relay(2)
    s_core.wait_recv()

    def add_spatial(q):
        x_at, y_at = q // 4, q % 4
        s_p[x_at, y_at] = (s_send[core, x_at, y_at].astype(F32) + s_rc[x_at, y_at].astype(F32)).astype(BF16)

    loop(0, planes, add_spatial)

    a_rows, b_rows = 2 * s_rows, s_rows

    def over_x(src, dst, group, k):
        slot = 4 * group + k
        return remote(src, dst, q_send_sem.at[slot], q_recv_sem.at[slot], at_x((x + k) % nx))

    def over_y(src, dst, group, k):
        slot = 4 * group + k
        return remote(src, dst, q_send_sem.at[slot], q_recv_sem.at[slot], at_y((y + k) % 4))

    def s_a_first(k):
        return over_x(s_p.at[(x + k) % nx, :, 0:a_rows], s_a1.at[k], 0, k)

    def s_b_first(k):
        return over_y(s_p.at[:, (y + k) % 4, a_rows : a_rows + b_rows], s_b1.at[k], 1, k)

    def s_a_second(k):
        return over_y(s_am.at[(y + k) % 4], s_a2.at[k], 2, k)

    def s_b_second(k):
        return over_x(s_bm.at[(x + k) % nx], s_b2.at[k], 3, k)

    loop(1, nx, lambda k: s_a_first(k).start())
    loop(1, 4, lambda k: s_b_first(k).start())

    @pl.when(y < 3)
    def _():
        halo_grad.wait_recv()

    @pl.when(y == 3)
    def _():
        sgp[half_rows] = jnp.zeros_like(sgp[half_rows])

    sbuf[half_cols : half_cols + 8] = jnp.zeros((8, mid), F32)

    def shift_row(i):
        sbuf[0:half_cols] = sgp[i].astype(F32)
        sgq[i] = sbuf[1 : 1 + half_cols].astype(BF16)

    loop(0, half_rows + 1, shift_row)
    here = sgp[0:half_rows].reshape(pix, mid)
    here_next = sgq[0:half_rows].reshape(pix, mid)

    def weave(row_par, col_par, value):
        value = value.reshape(half_rows, half_cols, mid)
        for i in range(half_rows):
            for block in range(mid // lanes):
                rg_s[2 * i + row_par, block, pl.ds(col_par, half_cols, stride=2), :] = value[
                    i, :, block * lanes : (block + 1) * lanes
                ]

    def tap(r, c):
        return ws[r, c * mid : (c + 1) * mid, :]

    weave(0, 0, dot_nt(here, tap(1, 1)))
    weave(0, 1, dot_nt(here, tap(1, 2)) + dot_nt(here_next, tap(1, 0)))
    below = sgp[1 : half_rows + 1].reshape(pix, mid)
    below_next = sgq[1 : half_rows + 1].reshape(pix, mid)
    weave(1, 0, dot_nt(here, tap(2, 1)) + dot_nt(below, tap(0, 1)))
    weave(
        1, 1,
        dot_nt(here, tap(2, 2)) + dot_nt(here_next, tap(2, 0)) + dot_nt(below, tap(0, 2)) + dot_nt(below_next, tap(0, 0)),
    )
    rterm[...] = jnp.zeros_like(rterm)

    def reduce_back(p):
        pre = pre_s[p]
        canvas = jnp.concatenate([rg_s[p, block] for block in range(mid // lanes)], axis=1)
        grad = (canvas * slope_of(pre, sigmoid(pre))).astype(BF16)
        rgp_s[p] = grad
        rterm[...] += dot_tn(img[p], grad)

    loop(0, rows, reduce_back)
    r_rows = chans // planes
    for h in range(2):
        for q in range(planes):
            r_send[h, q] = rterm[q * r_rows : (q + 1) * r_rows, h * lanes : (h + 1) * lanes].astype(BF16)
    loop(1, nx, lambda k: s_a_first(k).wait_recv())
    for y_at in range(4):
        total = s_p[x, y_at, 0:a_rows].astype(F32)
        for k in range(1, nx):
            total = total + s_a1[k, y_at].astype(F32)
        s_am[y_at] = total.astype(BF16)
    loop(1, 4, lambda k: s_a_second(k).start())
    loop(1, 4, lambda k: s_b_first(k).wait_recv())
    for x_at in range(nx):
        total = s_p[x_at, y, a_rows : a_rows + b_rows].astype(F32)
        for k in range(1, 4):
            total = total + s_b1[k, x_at].astype(F32)
        s_bm[x_at] = total.astype(BF16)
    loop(1, nx, lambda k: s_b_second(k).start())
    r_core = core_sum(r_send, r_rc, 9)
    r_core.start()

    r_core.wait_recv()
    add_core(r_send, r_rc, r_p)
    loop(1, planes, lambda k: plane_sum(r_p, r_rp, 2, k).start())

    def input_row(p):
        wide = dot_nt(rgp_s[p], wr[...])

        @pl.when(p % 2 == 1)
        def _():
            igrad[p] = wide.astype(BF16)

        @pl.when(p % 2 == 0)
        def _():
            first = pl.ds(pl.multiple_of((p // 2) * half_cols, half_cols), half_cols)
            for block in range(chans // lanes):
                lane = slice(block * lanes, (block + 1) * lanes)
                widebuf[block] = wide[:, lane]
                widebuf[block, pl.ds(0, half_cols, stride=2), :] = (
                    widebuf[block, pl.ds(0, half_cols, stride=2), :]
                    + stg[first, mid + block * lanes : mid + (block + 1) * lanes]
                )
                igrad[p, :, lane] = widebuf[block].astype(BF16)

    loop(0, rows, input_row)

    st_rows, rt_rows, t_rows = 3 * s_rows, r_rows, t_z.shape[0] * t_z.shape[1]
    total_a = s_am[y].astype(F32)
    for k in range(1, 4):
        s_a_second(k).wait_recv()
        total_a = total_a + s_a2[k].astype(F32)
    total_b = s_bm[x].astype(F32)
    for k in range(1, nx):
        s_b_second(k).wait_recv()
        total_b = total_b + s_b2[k].astype(F32)
    total = [total_a, total_b, plane_total(r_p, r_rp, 2)]
    if t_rows > st_rows + rt_rows:
        total.append(jnp.zeros((t_rows - st_rows - rt_rows, lanes), F32))
    t_z[...] = jnp.concatenate(total, axis=0).reshape(t_z.shape)
    loop(1, nz, lambda k: z_sum(t_z, t_rz, 2, k).start())

    out_y(2).start()

    for k in range(4):
        owner = e_owner(k)

        def e_add(j, total):
            e_sum(k, j).wait_recv()
            return total + e_rp[owner, j].astype(F32)

        e_z[owner] = lax.fori_loop(1, nz, e_add, e_p[owner, z].astype(F32)).reshape(e_z.shape[1:])

    def e_plane(k):
        place = (plane + k) % planes
        return remote(
            e_z.at[place % 4, place // 4], e_rz.at[k], p_send_sem.at[k], p_recv_sem.at[k], at_plane(place)
        )

    loop(1, planes, lambda k: e_plane(k).start())

    t_f[...] = z_total(t_z, t_rz, 2)
    loop(1, nz, lambda k: z_spread(t_f, t_g, 4, k).start())

    def e_total(k, total):
        e_plane(k).wait_recv()
        return total + e_rz[k]

    e_f[...] = lax.fori_loop(1, planes, e_total, e_z[y, x])

    def e_x(k):
        return remote(
            e_f, e_g.at[x], p_send_sem.at[3 * planes + k], p_recv_sem.at[3 * planes + k], at_x((x + k) % nx)
        )

    loop(1, nx, lambda k: e_x(k).start())

    loop(1, nz, lambda k: z_spread(t_f, t_g, 4, k).wait_recv())
    t_g[z] = t_f[...]
    t_out[core, x, y] = t_g[...].reshape(t_rows, lanes).astype(BF16)

    part_a, part_b = slice(0, a_rows), slice(a_rows, t_rows)

    def t_a_first(k):
        return over_y(t_out.at[core, x, y, part_a], t_out.at[core, x, y, part_a], 4, k)

    def t_b_first(k):
        return over_x(t_out.at[core, x, y, part_b], t_out.at[core, x, y, part_b], 5, k)

    def t_a_second(k):
        return over_x(t_out.at[core, x, :, part_a], t_out.at[core, x, :, part_a], 6, k)

    def t_b_second(k):
        return over_y(t_out.at[core, :, y, part_b], t_out.at[core, :, y, part_b], 7, k)

    def t_a_cross(k):
        at = t_out.at[core, (x + nx - k) % nx, :, part_a]
        return remote(at, at, c_send_sem.at[11 + k], c_recv_sem.at[11 + k], other_core)

    def t_b_cross(k):
        at = t_out.at[core, :, (y + 4 - k) % 4, part_b]
        return remote(at, at, c_send_sem.at[15 + k], c_recv_sem.at[15 + k], other_core)

    loop(1, 4, lambda k: t_a_first(k).start())
    loop(1, nx, lambda k: t_b_first(k).start())

    loop(1, 4, lambda k: t_a_first(k).wait_recv())
    loop(1, nx, lambda k: t_a_second(k).start())
    loop(1, nx, lambda k: t_b_first(k).wait_recv())
    loop(1, 4, lambda k: t_b_second(k).start())
    t_a_cross(0).start()
    t_b_cross(0).start()
    loop(1, nx, lambda k: e_x(k).wait_recv())
    e_g[x] = e_f[...]
    e_out[core, z] = e_g[...].reshape(e_rows, lanes).astype(BF16)

    def e_back(k):
        slot = nz + k
        return remote(
            e_out.at[core, z], e_out.at[core, z], z_send_sem.at[slot], z_recv_sem.at[slot], at_z((z + k) % nz)
        )

    loop(1, nz, lambda k: e_back(k).start())

    for k in (1, 3, 2):
        if k < nx:
            t_a_second(k).wait_recv()
            t_a_cross(k).start()
        t_b_second(k).wait_recv()
        t_b_cross(k).start()
    loop(1, nz, lambda k: e_back(k).wait())
    e_cross = remote(e_out.at[core], e_out.at[core], c_send_sem.at[10], c_recv_sem.at[10], other_core)
    e_cross.start()

    def finish_place(h, q):
        lane = slice(h * lanes, (h + 1) * lanes)
        for r in range(3):
            rows_at = pl.ds(pl.multiple_of(q * s_rows, s_rows), s_rows)
            sgrad[r, rows_at, lane] = t_out[h, q // 4, q % 4, r * s_rows : (r + 1) * s_rows].astype(F32) * scale
        rows_at = pl.ds(pl.multiple_of(q * r_rows, r_rows), r_rows)
        rgrad[rows_at, lane] = t_out[h, q // 4, q % 4, st_rows : st_rows + r_rows].astype(F32) * scale

    for h in range(2):

        @pl.when(core == h)
        def _():
            loop(0, planes, lambda q: finish_place(h, q))

    loop(0, nx, lambda k: t_a_cross(k).wait_recv())
    loop(0, 4, lambda k: t_b_cross(k).wait_recv())
    for h in range(2):

        @pl.when(core != h)
        def _():
            loop(0, planes, lambda q: finish_place(h, q))

    e_cross.wait_recv()
    for h in range(2):
        for z_at in range(nz):
            egrad[z_at * e_rows : (z_at + 1) * e_rows, h * lanes : (h + 1) * lanes] = e_out[h, z_at].astype(F32) * scale

    @pl.when(y < 3)
    def _():
        halo_row.wait_send()

    @pl.when(y > 0)
    def _():
        halo_grad.wait_send()

    def finish_y(k):
        weight_y(k).wait_send()
        cot_y(k).wait_send()
        out_y(k).wait()

    loop(1, 4, finish_y)
    for k in range(1, 4):
        loop(1, nx, lambda j: weight_x(k, j).wait_send())
        weight_core(k).wait_send()
    for copy in (s_core, r_core, e_cross):
        copy.wait_send()
    loop(1, nx, lambda k: e_x(k).wait_send())

    def finish_plane(k):
        e_plane(k).wait_send()
        plane_sum(r_p, r_rp, 2, k).wait_send()

    loop(1, planes, finish_plane)

    def finish_z(k):
        z_sum(t_z, t_rz, 2, k).wait_send()
        z_spread(t_f, t_g, 4, k).wait_send()

    loop(1, nz, finish_z)

    def finish_x(k):
        for copy in (s_a_first(k), s_b_second(k), t_b_first(k), t_a_second(k)):
            copy.wait_send()

    def finish_q(k):
        for copy in (s_b_first(k), s_a_second(k), t_a_first(k), t_b_second(k)):
            copy.wait_send()

    loop(1, nx, finish_x)
    loop(1, 4, finish_q)
    loop(0, nx, lambda k: t_a_cross(k).wait_send())
    loop(0, 4, lambda k: t_b_cross(k).wait_send())
    for k in range(4):
        e_core(k).wait_send()
        loop(1, nz, lambda j: e_sum(k, j).wait_send())


def place_kernel(cuts, *refs):
    count = len(cuts)
    sources, targets, sem = refs[:count], refs[count : 2 * count], refs[2 * count]
    copies = []
    for source, target, pieces in zip(sources, targets, cuts):
        size = source.shape[0] // pieces
        for piece in range(pieces):
            at = pl.ds(piece * size, size)
            copies.append(pltpu.make_async_copy(source.at[at], target.at[at], sem.at[len(copies)]))
    for copy in copies:
        copy.start()
    for copy in copies:
        copy.wait()


def body(nx, nz, images, reduce_weight, spatial_weight, expand_weight, cotangent):
    image = images[0]
    rows, cols, chans = image.shape
    mid = reduce_weight.shape[1]
    stack_ch, filt = expand_weight.shape
    half_rows, half_cols = rows // 2, cols // 2
    pix = half_rows * half_cols
    planes = nx * 4
    lanes = 128
    e_rows = stack_ch // nz
    f_rows = e_rows // nx
    s_rows = 9 * mid // planes
    a_rows, b_rows = s_rows // 3 * 2, s_rows // 3
    r_rows = chans // planes
    t_rows = -(-(s_rows + r_rows) // (8 * nz)) * 8 * nz
    cot_blocks = cotangent[0].reshape(4, pix, filt)
    weights = spatial_weight.reshape(3, 3 * mid, mid)
    vmem = pl.BlockSpec(memory_space=pltpu.VMEM)
    V = pltpu.VMEM
    D = pltpu.SemaphoreType.DMA
    scratch = [
        V(image.shape, BF16),
        V(reduce_weight.shape, BF16),
        V(weights.shape, BF16),
        V((4, pix, filt), F32),
        V((4, stack_ch, filt), BF16),
        V((4, pix, filt), BF16),
        V((2, half_rows + 1, half_cols, 3 * mid), BF16),
        V((rows, cols, mid), F32),
        V((mid // lanes, cols + 16, lanes), F32),
        V((pix, mid), F32),
        V((half_rows, half_cols, stack_ch), BF16),
        V((4, pix, filt), BF16),
        V((pix, stack_ch), F32),
        V((half_rows + 1, half_cols, mid), BF16),
        V((half_rows + 1, half_cols, mid), BF16),
        V((half_cols + 16, mid), F32),
        V((rows, mid // lanes, cols, lanes), F32),
        V((rows, cols, mid), BF16),
        V((chans, mid), F32),
        V((chans // lanes, cols, lanes), F32),
        V((2, 4, nz, e_rows, lanes), BF16),
        V((4, nz, e_rows, lanes), BF16),
        V((4, nz, e_rows, lanes), BF16),
        V((4, nz, e_rows, lanes), BF16),
        V((4, nx, f_rows, lanes), F32),
        V((planes, f_rows, lanes), F32),
        V((f_rows, lanes), F32),
        V((nx, f_rows, lanes), F32),
        V((2, nz, e_rows, lanes), BF16),
        V((2, nx, 4, s_rows, lanes), BF16),
        V((nx, 4, s_rows, lanes), BF16),
        V((nx, 4, s_rows, lanes), BF16),
        V((nx, 4, a_rows, lanes), BF16),
        V((4, a_rows, lanes), BF16),
        V((4, a_rows, lanes), BF16),
        V((4, nx, b_rows, lanes), BF16),
        V((nx, b_rows, lanes), BF16),
        V((nx, b_rows, lanes), BF16),
        V((2, planes, r_rows, lanes), BF16),
        V((planes, r_rows, lanes), BF16),
        V((planes, r_rows, lanes), BF16),
        V((planes, r_rows, lanes), BF16),
        V((nz, t_rows // nz, lanes), F32),
        V((nz, t_rows // nz, lanes), F32),
        V((t_rows // nz, lanes), F32),
        V((nz, t_rows // nz, lanes), F32),
        V((2, nx, 4, t_rows, lanes), BF16),
        D((14,)),
        D((14,)),
        D((5 * planes,)),
        D((5 * planes,)),
        D((5 * nz,)),
        D((5 * nz,)),
        D((19,)),
        D((19,)),
        D((4 * nx,)),
        D((4 * nx,)),
        D((4 * nz,)),
        D((4 * nz,)),
        D((32,)),
        D((32,)),
        D((rows + 4,)),
    ]
    results = pl.pallas_call(
        functools.partial(block_kernel, nx, nz),
        out_shape=(
            pltpu.VMEM((4, pix, filt), BF16),
            pltpu.VMEM(image.shape, BF16),
            pltpu.VMEM((chans, mid), F32),
            pltpu.VMEM((3, 3 * mid, mid), F32),
            pltpu.VMEM((stack_ch, filt), F32),
        ),
        in_specs=[pl.BlockSpec(memory_space=pltpu.HBM)] * 5,
        out_specs=[vmem] * 5,
        scratch_shapes=scratch,
        compiler_params=pltpu.CompilerParams(
            collective_id=0, has_side_effects=True, vmem_limit_bytes=48 * 1024 * 1024
        ),
    )(image, reduce_weight, weights, expand_weight, cot_blocks)
    cuts = (2, 4, 1, 3, 2)
    output, input_grad, reduce_grad, spatial_grad, expand_grad = pl.pallas_call(
        functools.partial(place_kernel, cuts),
        out_shape=[jax.ShapeDtypeStruct(result.shape, result.dtype) for result in results],
        in_specs=[pl.BlockSpec(memory_space=pl.ANY)] * 5,
        out_specs=[pl.BlockSpec(memory_space=pl.ANY)] * 5,
        scratch_shapes=[D((sum(cuts),))],
        compiler_params=pltpu.CompilerParams(vmem_limit_bytes=2 * 1024 * 1024),
    )(*results)
    return (
        output.reshape((1, 4 * half_rows, half_cols, filt)),
        input_grad[None],
        reduce_grad,
        spatial_grad.reshape(3, 3, mid, mid),
        expand_grad,
    )


def solution(mesh):
    nx = 4 if mesh.shape["dp"] >= 32 else 2
    nz = mesh.shape["dp"] // (2 * nx)
    return jax.shard_map(
        functools.partial(body, nx, nz),
        mesh=mesh,
        in_specs=(
            P("dp", ("space", "chan"), None, None),
            P(),
            P(),
            P(None, ("space", "chan")),
            P("dp", None, None, ("space", "chan")),
        ),
        out_specs=(
            P("dp", None, None, ("space", "chan")),
            P("dp", ("space", "chan"), None, None),
            P(),
            P(),
            P(None, ("space", "chan")),
        ),
        check_vma=False,
    )
```
